128 devices in a mesh: row: 8 (over z_lo, x), col: 16 (over z_hi, y, core).
Axes of the slice: x: 4, y: 4, z: 4 (z_hi: 2, z_lo: 2; z = z_hi * 2 + z_lo), core: 2. Of those that a mesh axis runs over, the one named last changes fastest.
Arguments:
- hessian: float32 [8192, 24576], P('row', 'col'), may hold values from -62 to 62
- block_order: int32 [16, 16], P('col'), may hold values from 0 to 15, each once within a row
- send_slot: int32 [4, 128], P(None, 'col'), may hold values from 0 to 1
Outputs:
- rotated: float32 [8192, 24576], P('row', 'col')
The draws below stay inside these ranges and needn't reach their ends.
Inputs may be any that keep to these rules, and one draw needn't show every extreme that they name: `block_order`: each row is a permutation.
All inputs are finite; a program needn't handle non-finite values.
Results may differ from the reference program's by a relative error of at most 0.00035.
Values sent between devices are 32-bit elements; how exact they have to be, the bound alone decides.
A program may use at most 128 MiB of HBM per device.

```python
import math
import jax
import jax.numpy as jnp
import numpy as np
from jax import lax

ROWS = 8192
BW = 96
STEPS = 4
INNER = 2
NPAIR = 128
GBLK = 16
NCOLS = 24576
N_ROW = 8
N_COL = 16


def draw_hessian(key, part):
    key_base = jax.random.fold_in(key, 11)
    key_rows = jax.random.fold_in(key, 23)
    key_cols = jax.random.fold_in(key, 37)
    row_scale = jnp.exp(jax.random.uniform(key_rows, (ROWS, 1), jnp.float32, 0.0, math.log(3.5)))
    col_scale = jnp.exp(jax.random.uniform(key_cols, (1, NCOLS), jnp.float32, 0.0, math.log(3.5)))
    base = jax.random.truncated_normal(key_base, -5.0, 5.0, (ROWS, NCOLS), jnp.float32)
    return (base * row_scale * col_scale).astype(jnp.float32)


def plant(drawn, key, smallest, high):
    spot = [jax.random.randint(jax.random.fold_in(key, axis), (), 0, length) for axis, length in enumerate(drawn.shape)]
    widest = drawn.shape.index(max(drawn.shape))
    beside = spot[:widest] + [(spot[widest] + 1) % drawn.shape[widest]] + spot[widest + 1:]
    return drawn.at[tuple(spot)].set(smallest).at[tuple(beside)].set(high)


def setup_inputs(seed: int = 0) -> dict:
    arg_keys = jax.random.split(jax.random.key(seed), 4)
    hessian = draw_hessian(jax.random.fold_in(arg_keys[3], 71), 0)
    block_order = jax.vmap(lambda own: jax.random.permutation(own, GBLK))(jax.random.split(arg_keys[1], N_COL)).reshape((N_COL, GBLK)).astype(jnp.int32)
    send_slot = plant(jax.random.randint(arg_keys[2], (STEPS, NPAIR), 0, 2), jax.random.fold_in(arg_keys[2], 1), 0, 1).astype(jnp.int32)
    return dict(hessian=hessian, block_order=block_order, send_slot=send_slot)


def lower_solve(lower_factor, basis):
    solved = jax.scipy.linalg.solve_triangular(lower_factor, jnp.transpose(basis), lower=True)
    return jnp.transpose(solved)

def rotation(gram_matrix):
    pair_width = gram_matrix.shape[-1]
    scale = jnp.sqrt(lax.optimization_barrier(jnp.sum(gram_matrix * gram_matrix, axis=(1, 2), keepdims=True)))
    current = jnp.broadcast_to(jnp.eye(pair_width, dtype=gram_matrix.dtype), gram_matrix.shape)
    for repeat in range(INNER):
        basis = jnp.einsum('pab,pbc->pac', gram_matrix, current, precision=lax.Precision.HIGHEST) / scale
        cross = jnp.einsum('pka,pkb->pab', basis, basis, precision=lax.Precision.HIGHEST)
        factor = jnp.linalg.cholesky(cross)
        current = jax.vmap(lower_solve)(factor, basis)
    return current

def reference(hessian, block_order, send_slot):
    total_rows = hessian.shape[0]
    blocks = hessian.reshape(total_rows, N_COL, GBLK, BW)
    blocks = jnp.take_along_axis(blocks, block_order.astype(jnp.int32)[None, :, :, None], axis=2)
    pairs = blocks.reshape(total_rows, NPAIR, 2 * BW)
    col_bits = N_COL.bit_length() - 1
    for step_index in range(STEPS):
        gram_matrix = jnp.einsum('rpa,rpb->pab', pairs, pairs, precision=lax.Precision.HIGHEST)
        rotator = rotation(gram_matrix)
        pairs = jnp.einsum('rpa,pab->rpb', pairs, rotator, precision=lax.Precision.HIGHEST)
        slots = pairs.reshape(total_rows, NPAIR, 2, BW)
        slot_zero = slots[:, :, 0]
        slot_one = slots[:, :, 1]
        chosen = (send_slot[step_index] == 0)[None, :, None]
        outgoing = jnp.where(chosen, slot_zero, slot_one)
        partner = (np.arange(NPAIR) ^ N_ROW << step_index % col_bits).astype(np.int32)
        incoming = outgoing[:, jnp.asarray(partner)]
        slot_zero = jnp.where(chosen, incoming, slot_zero)
        slot_one = jnp.where(chosen, slot_one, incoming)
        pairs = jnp.stack([slot_zero, slot_one], axis=2).reshape(total_rows, NPAIR, 2 * BW)
    return pairs.reshape(total_rows, NCOLS)
```

```python
import jax
import jax.numpy as jnp
from jax import lax
from jax.experimental import pallas as pl
from jax.experimental.pallas import tpu as pltpu
from jax.sharding import PartitionSpec as P

BW = 96
STEPS = 4
INNER = 2


def swapped(value, axis, stride):
    mask = 2**stride
    pairs = [(source, source ^ mask) for source in range(lax.axis_size(axis))]
    return lax.ppermute(value, axis, pairs)


F32=jnp.float32; BF=jnp.bfloat16
W=192
def pieces(x):
    h=x.astype(BF); r=x-h.astype(F32); m=r.astype(BF); l=(r-m.astype(F32)).astype(BF)
    return h,m,l
def outer(left, right):
    a0,a1,a2=pieces(left); b0,b1,b2=pieces(right)
    a=jnp.concatenate([a2,a0,a1,a1,a0,a0],0)
    b=jnp.concatenate([b0,b2,b1,b0,b1,b0],0)
    return lax.dot_general(a,b,(((0,),(0,)),((),())),preferred_element_type=F32)
def rsqrt(d):
    r=lax.rsqrt(d)
    return r*(1.5-0.5*d*r*r)
def eliminate(rows, base, NB):
    diag=rows[0][:,base:base+NB]
    cols=[jnp.broadcast_to(diag[:,c:c+1],(NB,128)) for c in range(NB)]
    idx=lax.broadcasted_iota(jnp.int32,(NB,128),0)
    rows=[[r[:,i:i+128] for i in range(0,r.shape[1],128)] for r in rows]
    for c in range(NB):
        col=cols[c]
        r=rsqrt(jnp.broadcast_to(col[c:c+1],(NB,128)))
        l=col*r
        lm=jnp.where(idx>c,l,0.0)
        for q in range(c+1,NB):
            cols[q]=cols[q]-lm*jnp.broadcast_to(l[q:q+1],(NB,128))
        for g in rows:
            for i in range(len(g)):
                u=jnp.broadcast_to(g[i][c:c+1],(NB,128))*r
                g[i]=jnp.where(idx==c,u,g[i]-lm*u)
    return [jnp.concatenate(g,1) if len(g)>1 else g[0] for g in rows]
def factor(a_ref, e_ref, NB):
    for t in range(W//NB):
        j=t*NB
        lo=(j//128)*128
        panel=[a_ref[j:j+NB,lo:]]
        if e_ref is not None: panel.append(e_ref[j:j+NB,:])
        out=eliminate(panel,j-lo,NB)
        u=out[0]
        ri=lax.broadcasted_iota(jnp.int32,u.shape,0)+(j-lo)
        ci=lax.broadcasted_iota(jnp.int32,u.shape,1)
        u=jnp.where(ci>=ri,u,0.0)
        a_ref[j:j+NB,lo:]=u
        if lo: a_ref[j:j+NB,:lo]=jnp.zeros((NB,lo),F32)
        if e_ref is not None: e_ref[j:j+NB,:]=out[1]
        rem=W-j-NB
        if rem==0: break
        left=u[:,j+NB-lo:W-lo]
        a_ref[j+NB:W,lo:]=a_ref[j+NB:W,lo:]-outer(left,u)
        if e_ref is not None:
            e_ref[j+NB:W,:]=e_ref[j+NB:W,:]-outer(left,out[1])
def rotate(g, a_ref, e_ref, NB):
    s=jnp.sum(jnp.sum(g*g,axis=0,keepdims=True),axis=1,keepdims=True)
    y=g/jnp.sqrt(s)
    yy=y[:,:W]
    a_ref[:,:W]=lax.dot_general(yy,yy,(((0,),(0,)),((),())),precision=lax.Precision.HIGHEST,preferred_element_type=F32)
    a_ref[:,W:]=jnp.zeros((W,256-W),F32)
    factor(a_ref,None,NB)
    u=a_ref[...]
    e_ref[...]=u
    uu=u[:,:W]
    a_ref[:,:W]=lax.dot_general(uu,uu,(((1,),(1,)),((),())),precision=lax.Precision.HIGHEST,preferred_element_type=F32)
    a_ref[:,W:]=jnp.zeros((W,256-W),F32)
    factor(a_ref,e_ref,NB)

def rotation_kernel(gram_ref, turn_ref, a_ref, e_ref):
    a_ref[...] = jnp.zeros((W, 256), F32)
    a_ref[:, :W] = gram_ref[0]
    rotate(a_ref[...], a_ref, e_ref, 32)
    turn_ref[0] = e_ref[:, :W]


def rotation(gram_matrix):
    return pl.pallas_call(
        rotation_kernel,
        out_shape=jax.ShapeDtypeStruct((1, W, W), F32),
        in_specs=[pl.BlockSpec(memory_space=pltpu.VMEM)],
        out_specs=pl.BlockSpec(memory_space=pltpu.VMEM),
        scratch_shapes=[pltpu.VMEM((W, 256), F32), pltpu.VMEM((W, 256), F32)],
        compiler_params=pltpu.CompilerParams(vmem_limit_bytes=16 * 2**20),
        name="rotation",
    )(gram_matrix)


def swap_step(pairs, chosen_slots, swap_bit):
    local_rows, pair_count, pair_width = pairs.shape
    slots = pairs.reshape(local_rows, pair_count, 2, pair_width // 2)
    slot_zero = slots[:, :, 0]
    slot_one = slots[:, :, 1]
    chosen = (chosen_slots == 0)[None, :, None]
    outgoing = jnp.where(chosen, slot_zero, slot_one)
    incoming = swapped(outgoing, "col", swap_bit)
    slot_zero = jnp.where(chosen, incoming, slot_zero)
    slot_one = jnp.where(chosen, slot_one, incoming)
    return jnp.stack([slot_zero, slot_one], axis=2).reshape(local_rows, pair_count, pair_width)


def body(hessian, block_order, send_slot):
    local_rows, local_cols = hessian.shape
    row_count = lax.axis_size("row")
    col_bits = lax.axis_size("col").bit_length() - 1
    row_index = lax.axis_index("row")
    blocks = hessian.reshape(local_rows, local_cols // BW, BW)
    blocks = jnp.take(blocks, block_order[0], axis=1)
    local_pairs = blocks.reshape(local_rows, row_count, 2 * BW)
    full_pairs = lax.all_to_all(local_pairs, "row", split_axis=1, concat_axis=0, tiled=True)
    own_sends = lax.dynamic_slice_in_dim(send_slot, row_index, 1, 1)
    for step_index in range(STEPS):
        gram_matrix = jnp.einsum(
            "rpa,rpb->pab", full_pairs, full_pairs, precision=lax.Precision.HIGHEST
        )
        rotator = rotation(gram_matrix)
        full_pairs = jnp.einsum(
            "rpa,pba->rpb", full_pairs, rotator, precision=lax.Precision.HIGHEST
        )
        full_pairs = swap_step(full_pairs, own_sends[step_index], step_index % col_bits)
    result = lax.all_to_all(full_pairs, "row", split_axis=0, concat_axis=1, tiled=True)
    return result.reshape(local_rows, local_cols)


def solution(mesh):
    in_specs = (P("row", "col"), P("col", None), P(None, "col"))
    out_specs = P("row", "col")
    return jax.shard_map(body, mesh=mesh, in_specs=in_specs, out_specs=out_specs, check_vma=False)
```

```python
import functools

import jax
import jax.numpy as jnp
from jax import lax
from jax.experimental import pallas as pl
from jax.experimental.pallas import tpu as pltpu
from jax.sharding import PartitionSpec as P

MESH = pl.DeviceIdType.MESH
BW = 96
F32=jnp.float32; BF=jnp.bfloat16
W=192
def pieces(x):
    h=x.astype(BF); r=x-h.astype(F32); m=r.astype(BF); l=(r-m.astype(F32)).astype(BF)
    return h,m,l
def outer(left, right):
    a0,a1,a2=pieces(left); b0,b1,b2=pieces(right)
    a=jnp.concatenate([a2,a0,a1,a1,a0,a0],0)
    b=jnp.concatenate([b0,b2,b1,b0,b1,b0],0)
    return lax.dot_general(a,b,(((0,),(0,)),((),())),preferred_element_type=F32)
def rsqrt(d):
    r=lax.rsqrt(d)
    return r*(1.5-0.5*d*r*r)
def eliminate(rows, base, NB):
    diag=rows[0][:,base:base+NB]
    cols=[jnp.broadcast_to(diag[:,c:c+1],(NB,128)) for c in range(NB)]
    idx=lax.broadcasted_iota(jnp.int32,(NB,128),0)
    rows=[[r[:,i:i+128] for i in range(0,r.shape[1],128)] for r in rows]
    for c in range(NB):
        col=cols[c]
        r=rsqrt(jnp.broadcast_to(col[c:c+1],(NB,128)))
        l=col*r
        lm=jnp.where(idx>c,l,0.0)
        for q in range(c+1,NB):
            cols[q]=cols[q]-lm*jnp.broadcast_to(l[q:q+1],(NB,128))
        for g in rows:
            for i in range(len(g)):
                u=jnp.broadcast_to(g[i][c:c+1],(NB,128))*r
                g[i]=jnp.where(idx==c,u,g[i]-lm*u)
    return [jnp.concatenate(g,1) if len(g)>1 else g[0] for g in rows]
def factor(a_ref, e_ref, NB):
    for t in range(W//NB):
        j=t*NB
        lo=(j//128)*128
        panel=[a_ref[j:j+NB,lo:]]
        if e_ref is not None: panel.append(e_ref[j:j+NB,:])
        out=eliminate(panel,j-lo,NB)
        u=out[0]
        ri=lax.broadcasted_iota(jnp.int32,u.shape,0)+(j-lo)
        ci=lax.broadcasted_iota(jnp.int32,u.shape,1)
        u=jnp.where(ci>=ri,u,0.0)
        a_ref[j:j+NB,lo:]=u
        if lo: a_ref[j:j+NB,:lo]=jnp.zeros((NB,lo),F32)
        if e_ref is not None: e_ref[j:j+NB,:]=out[1]
        rem=W-j-NB
        if rem==0: break
        left=u[:,j+NB-lo:W-lo]
        a_ref[j+NB:W,lo:]=a_ref[j+NB:W,lo:]-outer(left,u)
        if e_ref is not None:
            e_ref[j+NB:W,:]=e_ref[j+NB:W,:]-outer(left,out[1])
def rotate(g, a_ref, e_ref, NB):
    s=jnp.sum(jnp.sum(g*g,axis=0,keepdims=True),axis=1,keepdims=True)
    y=g/jnp.sqrt(s)
    yy=y[:,:W]
    a_ref[:,:W]=lax.dot_general(yy,yy,(((0,),(0,)),((),())),precision=lax.Precision.HIGHEST,preferred_element_type=F32)
    a_ref[:,W:]=jnp.zeros((W,256-W),F32)
    factor(a_ref,None,NB)
    u=a_ref[...]
    e_ref[...]=u
    uu=u[:,:W]
    a_ref[:,:W]=lax.dot_general(uu,uu,(((1,),(1,)),((),())),precision=lax.Precision.HIGHEST,preferred_element_type=F32)
    a_ref[:,W:]=jnp.zeros((W,256-W),F32)
    factor(a_ref,e_ref,NB)
STEPS = 4
ROWS_LOCAL = 1024
VMEM_LIMIT = 60 * 2**20


def split_two(x):
    high = x.astype(BF)
    return high, (x - high.astype(F32)).astype(BF)


def pack_gram(gram, ref):
    ref[0:W, :] = gram[:, 0:128]
    ref[W : W + 64, :] = jnp.concatenate([gram[128:W, 128:W], jnp.zeros((64, 64), F32)], 1)


def unpack_gram(packed):
    right = jnp.concatenate([jnp.transpose(packed[128:W, :]), packed[W : W + 64, 0:64]], 0)
    return jnp.concatenate([packed[0:W, :], right], 1)


def swap_rows(x):
    return jnp.concatenate([x[BW:], x[:BW]], 0)


def swap_columns(x):
    return jnp.concatenate([x[:, BW:], x[:, :BW]], 1)


def pair_kernel(
    pairs, slot_ref, first_ref, second_ref, kept_out, came_out,
    kept, came, leaving, gram_out, gram_in, turn, a_ref, e_ref,
    gram_sent, gram_came, turn_sent, turn_came, block_sent, block_came, local_sem,
):
    row = lax.axis_index("row")
    col = lax.axis_index("col")
    half = pairs // 2

    def partner(step):
        stride = (step * step * step + 5 * step + 6) // 6
        return col + stride * (1 - 2 * ((col // stride) % 2))

    barrier = pltpu.get_barrier_semaphore()
    for shift in range(1, pairs):
        pl.semaphore_signal(barrier, inc=1, device_id=((row + shift) % pairs, col), device_id_type=MESH)
    for step in range(STEPS):
        pl.semaphore_signal(barrier, inc=1, device_id=(row, partner(step)), device_id_type=MESH)

    load_first = pltpu.make_async_copy(first_ref, kept, local_sem.at[0])
    load_second = pltpu.make_async_copy(second_ref, came.at[0], local_sem.at[1])
    load_first.start()
    load_second.start()
    load_first.wait()
    load_second.wait()
    pl.semaphore_wait(barrier, pairs - 1 + STEPS)

    def gram_copy(step, pair):
        return pltpu.make_async_remote_copy(
            src_ref=gram_out.at[pair], dst_ref=gram_in.at[step, row], send_sem=gram_sent.at[pair],
            recv_sem=gram_came.at[step, row], device_id=(pair, col), device_id_type=MESH)

    def gram_arrival(step, source):
        return pltpu.make_async_remote_copy(
            src_ref=gram_out.at[source], dst_ref=gram_in.at[step, source], send_sem=gram_sent.at[source],
            recv_sem=gram_came.at[step, source], device_id=(source, col), device_id_type=MESH)

    def turn_copy(step, target):
        return pltpu.make_async_remote_copy(
            src_ref=turn.at[step, row], dst_ref=turn.at[step, row], send_sem=turn_sent.at[target],
            recv_sem=turn_came.at[step, row], device_id=(target, col), device_id_type=MESH)

    def turn_arrival(step, pair):
        return pltpu.make_async_remote_copy(
            src_ref=turn.at[step, pair], dst_ref=turn.at[step, pair], send_sem=turn_sent.at[pair],
            recv_sem=turn_came.at[step, pair], device_id=(pair, col), device_id_type=MESH)

    def block_copy(step, pair):
        return pltpu.make_async_remote_copy(
            src_ref=leaving.at[pair], dst_ref=came.at[step + 1, pair], send_sem=block_sent.at[pair],
            recv_sem=block_came.at[step, pair], device_id=(row, partner(step)), device_id_type=MESH)

    def load_pair(step, pair):
        return split_two(jnp.concatenate([kept[pair], came[step, pair]], 0))

    def phase(index, _):
        split = jnp.minimum(index // 2, 1)
        step = (1 - split) * index + split * (2 + (index - 2) // 2)
        start = split * half * (index % 2)
        count = pairs - split * half
        mine = (row >= start) & (row < start + count)

        def gram_one(pair, _):
            @pl.when(step > 0)
            def _():
                block_copy(step - 1, pair).wait_recv()

            high, low = load_pair(step, pair)
            gram = lax.dot_general(
                jnp.concatenate([low, high, high], 1), jnp.concatenate([high, low, high], 1),
                (((1,), (1,)), ((), ())), preferred_element_type=F32)

            @pl.when(pair == row)
            def _():
                pack_gram(gram, gram_in.at[step, row])

            @pl.when(pair != row)
            def _():
                pack_gram(gram, gram_out.at[pair])
                gram_copy(step, pair).start()

            return 0

        lax.fori_loop(start, start + count, gram_one, 0)

        @pl.when(mine)
        def _():
            def arrive(shift, _):
                gram_arrival(step, (row + shift) % pairs).wait_recv()
                return 0

            lax.fori_loop(1, pairs, arrive, 0)
            total = gram_in[step, 0]
            for source in range(1, pairs):
                total = total + gram_in[step, source]
            gram = unpack_gram(total)
            came_first = (step > 0) & (slot_ref[jnp.maximum(step - 1, 0), row] == 0)
            gram = jnp.where(came_first, swap_columns(swap_rows(gram)), gram)
            rotate(gram, a_ref, e_ref, 32)
            turned = e_ref[:, :W]
            turned = jnp.where(came_first, swap_columns(turned), turned)
            turned = jnp.where(slot_ref[step, row] == 0, swap_rows(turned), turned)
            own = turn.at[step, row]
            own[0:W, :] = turned[:, 0:128]
            own[W:, :] = jnp.concatenate([turned[0:BW, 128:W], turned[BW:W, 128:W]], 1)

            def send(shift, _):
                turn_copy(step, (row + shift) % pairs).start()
                return 0

            lax.fori_loop(1, pairs, send, 0)

        def update_one(pair, _):
            @pl.when(pair != row)
            def _():
                turn_arrival(step, pair).wait_recv()
                gram_copy(step, pair).wait_send()

            @pl.when(step > 0)
            def _():
                block_copy(step - 1, pair).wait_send()

            packed = turn[step, pair]
            tail = packed[W:, :]
            turned = jnp.concatenate(
                [packed[0:W, :], jnp.concatenate([tail[:, 0:64], tail[:, 64:128]], 0)], 1)
            turn_high, turn_low = split_two(turned)
            high, low = load_pair(step, pair)
            dims = (((1,), (0,)), ((), ()))
            new = (
                lax.dot_general(turn_low, high, dims, preferred_element_type=F32)
                + lax.dot_general(turn_high, low, dims, preferred_element_type=F32)
                + lax.dot_general(turn_high, high, dims, preferred_element_type=F32))
            kept[pair] = new[0:BW]
            leaving[pair] = new[BW:]
            block_copy(step, pair).start()
            return 0

        lax.fori_loop(start, start + count, update_one, 0)

        @pl.when(mine)
        def _():
            def sent(shift, _):
                turn_copy(step, (row + shift) % pairs).wait_send()
                return 0

            lax.fori_loop(1, pairs, sent, 0)

        return 0

    lax.fori_loop(0, 6, phase, 0)

    store_kept = pltpu.make_async_copy(kept, kept_out, local_sem.at[0])
    store_kept.start()

    def finish(pair, _):
        block_copy(STEPS - 1, pair).wait()
        return 0

    lax.fori_loop(0, pairs, finish, 0)
    store_came = pltpu.make_async_copy(came.at[STEPS], came_out, local_sem.at[1])
    store_came.start()
    store_kept.wait()
    store_came.wait()


def pair_steps(send_slot, first, second):
    pairs, width, rows = first.shape
    block = jax.ShapeDtypeStruct(first.shape, F32)
    dma = pltpu.SemaphoreType.DMA
    return pl.pallas_call(
        functools.partial(pair_kernel, pairs),
        out_shape=[block, block],
        in_specs=[
            pl.BlockSpec(memory_space=pltpu.SMEM),
            pl.BlockSpec(memory_space=pl.ANY),
            pl.BlockSpec(memory_space=pl.ANY),
        ],
        out_specs=[pl.BlockSpec(memory_space=pl.ANY)] * 2,
        scratch_shapes=[
            pltpu.VMEM((pairs, width, rows), F32),
            pltpu.VMEM((STEPS + 1, pairs, width, rows), F32),
            pltpu.VMEM((pairs, width, rows), F32),
            pltpu.VMEM((pairs, 256, 128), F32),
            pltpu.VMEM((STEPS, pairs, 256, 128), F32),
            pltpu.VMEM((STEPS, pairs, 288, 128), F32),
            pltpu.VMEM((W, 256), F32),
            pltpu.VMEM((W, 256), F32),
            dma((pairs,)),
            dma((STEPS, pairs)),
            dma((pairs,)),
            dma((STEPS, pairs)),
            dma((pairs,)),
            dma((STEPS, pairs)),
            dma((2,)),
        ],
        compiler_params=pltpu.CompilerParams(
            collective_id=0, has_side_effects=True, vmem_limit_bytes=VMEM_LIMIT),
        name="pair_steps",
    )(send_slot, first, second)


def gather_kernel(order_ref, hessian_ref, first_ref, second_ref, turned):
    chunk = hessian_ref.shape[0]
    for part in range(hessian_ref.shape[1] // 384):
        turned[4 * part : 4 * part + 4] = jnp.transpose(
            hessian_ref[:, 384 * part : 384 * part + 384]).reshape(4, BW, chunk)
    for pair in range(first_ref.shape[0]):
        first_ref[pair] = turned[order_ref[0, 2 * pair]]
        second_ref[pair] = turned[order_ref[0, 2 * pair + 1]]


def gathered(hessian, block_order):
    rows, columns = hessian.shape
    blocks = columns // BW
    chunk = 256
    shape = jax.ShapeDtypeStruct((blocks // 2, BW, rows), F32)
    spec = pl.BlockSpec((blocks // 2, BW, chunk), lambda i: (0, 0, i))
    return pl.pallas_call(
        gather_kernel,
        grid=(rows // chunk,),
        out_shape=[shape, shape],
        in_specs=[
            pl.BlockSpec(memory_space=pltpu.SMEM),
            pl.BlockSpec((chunk, columns), lambda i: (i, 0)),
        ],
        out_specs=[spec, spec],
        scratch_shapes=[pltpu.VMEM((blocks, BW, chunk), F32)],
        compiler_params=pltpu.CompilerParams(vmem_limit_bytes=32 * 2**20),
        name="gathered",
    )(block_order, hessian)


def scatter_kernel(slot_ref, kept_ref, came_ref, out_ref):
    for pair in range(0, kept_ref.shape[0], 2):
        parts = []
        for each in (pair, pair + 1):
            came_first = slot_ref[STEPS - 1, each] == 0
            kept, came = kept_ref[each], came_ref[each]
            parts += [jnp.where(came_first, came, kept), jnp.where(came_first, kept, came)]
        out_ref[:, 192 * pair : 192 * pair + 384] = jnp.transpose(jnp.concatenate(parts, 0))


def scattered(send_slot, kept, came):
    pairs, width, rows = kept.shape
    chunk = 256
    spec = pl.BlockSpec((pairs, width, chunk), lambda i: (0, 0, i))
    return pl.pallas_call(
        scatter_kernel,
        grid=(rows // chunk,),
        out_shape=jax.ShapeDtypeStruct((rows, pairs * 2 * width), F32),
        in_specs=[pl.BlockSpec(memory_space=pltpu.SMEM), spec, spec],
        out_specs=pl.BlockSpec((chunk, pairs * 2 * width), lambda i: (i, 0)),
        compiler_params=pltpu.CompilerParams(vmem_limit_bytes=32 * 2**20),
        name="scattered",
    )(send_slot, kept, came)


def body(hessian, block_order, send_slot):
    first, second = gathered(hessian, block_order)
    kept, came = pair_steps(send_slot, first, second)
    return scattered(send_slot, kept, came)


def solution(mesh):
    in_specs = (P("row", "col"), P("col", None), P(None, "col"))
    out_specs = P("row", "col")
    return jax.shard_map(body, mesh=mesh, in_specs=in_specs, out_specs=out_specs, check_vma=False)
```

```python
import functools

import jax
import jax.numpy as jnp
from jax import lax
from jax.experimental import pallas as pl
from jax.experimental.pallas import tpu as pltpu
from jax.sharding import PartitionSpec as P

MESH = pl.DeviceIdType.MESH
BW = 96
F32=jnp.float32; BF=jnp.bfloat16
W=192
def pieces(x):
    h=x.astype(BF); r=x-h.astype(F32); m=r.astype(BF); l=(r-m.astype(F32)).astype(BF)
    return h,m,l
def outer(left, right):
    a0,a1,a2=pieces(left); b0,b1,b2=pieces(right)
    a=jnp.concatenate([a2,a0,a1,a1,a0,a0],0)
    b=jnp.concatenate([b0,b2,b1,b0,b1,b0],0)
    return lax.dot_general(a,b,(((0,),(0,)),((),())),preferred_element_type=F32)
def rsqrt(d):
    r=lax.rsqrt(d)
    return r*(1.5-0.5*d*r*r)
def eliminate(rows, base, NB):
    diag=rows[0][:,base:base+NB]
    cols=[jnp.broadcast_to(diag[:,c:c+1],(NB,128)) for c in range(NB)]
    idx=lax.broadcasted_iota(jnp.int32,(NB,128),0)
    rows=[[r[:,i:i+128] for i in range(0,r.shape[1],128)] for r in rows]
    for c in range(NB):
        col=cols[c]
        r=rsqrt(jnp.broadcast_to(col[c:c+1],(NB,128)))
        l=col*r
        lm=jnp.where(idx>c,l,0.0)
        for q in range(c+1,NB):
            cols[q]=cols[q]-lm*jnp.broadcast_to(l[q:q+1],(NB,128))
        for g in rows:
            for i in range(len(g)):
                u=jnp.broadcast_to(g[i][c:c+1],(NB,128))*r
                g[i]=jnp.where(idx==c,u,g[i]-lm*u)
    return [jnp.concatenate(g,1) if len(g)>1 else g[0] for g in rows]
def factor(a_ref, e_ref, NB):
    for t in range(W//NB):
        j=t*NB
        lo=(j//128)*128
        panel=[a_ref[j:j+NB,lo:]]
        if e_ref is not None: panel.append(e_ref[j:j+NB,:])
        out=eliminate(panel,j-lo,NB)
        u=out[0]
        ri=lax.broadcasted_iota(jnp.int32,u.shape,0)+(j-lo)
        ci=lax.broadcasted_iota(jnp.int32,u.shape,1)
        u=jnp.where(ci>=ri,u,0.0)
        a_ref[j:j+NB,lo:]=u
        if lo: a_ref[j:j+NB,:lo]=jnp.zeros((NB,lo),F32)
        if e_ref is not None: e_ref[j:j+NB,:]=out[1]
        rem=W-j-NB
        if rem==0: break
        left=u[:,j+NB-lo:W-lo]
        a_ref[j+NB:W,lo:]=a_ref[j+NB:W,lo:]-outer(left,u)
        if e_ref is not None:
            e_ref[j+NB:W,:]=e_ref[j+NB:W,:]-outer(left,out[1])
def rotate(g, a_ref, e_ref, NB):
    s=jnp.sum(jnp.sum(g*g,axis=0,keepdims=True),axis=1,keepdims=True)
    y=g/jnp.sqrt(s)
    yy=y[:,:W]
    a_ref[:,:W]=lax.dot_general(yy,yy,(((0,),(0,)),((),())),precision=lax.Precision.HIGHEST,preferred_element_type=F32)
    a_ref[:,W:]=jnp.zeros((W,256-W),F32)
    factor(a_ref,None,NB)
    u=a_ref[...]
    e_ref[...]=u
    uu=u[:,:W]
    a_ref[:,:W]=lax.dot_general(uu,uu,(((1,),(1,)),((),())),precision=lax.Precision.HIGHEST,preferred_element_type=F32)
    a_ref[:,W:]=jnp.zeros((W,256-W),F32)
    factor(a_ref,e_ref,NB)
STEPS = 4
ROWS_LOCAL = 1024
VMEM_LIMIT = 60 * 2**20


def split_two(x):
    high = x.astype(BF)
    return high, (x - high.astype(F32)).astype(BF)


def pack_gram(gram, ref):
    ref[0:W, :] = gram[:, 0:128]
    ref[W : W + 64, :] = jnp.concatenate([gram[128:W, 128:W], jnp.zeros((64, 64), F32)], 1)


def unpack_gram(packed):
    right = jnp.concatenate([jnp.transpose(packed[128:W, :]), packed[W : W + 64, 0:64]], 0)
    return jnp.concatenate([packed[0:W, :], right], 1)


def swap_rows(x):
    return jnp.concatenate([x[BW:], x[:BW]], 0)


def swap_columns(x):
    return jnp.concatenate([x[:, BW:], x[:, :BW]], 1)


def pair_kernel(
    pairs, slot_ref, first_ref, second_ref, kept_out, came_out,
    kept, came, leaving, gram_out, gram_in, turn, a_ref, e_ref,
    gram_sent, gram_came, turn_sent, turn_came, block_sent, block_came, local_sem,
):
    row = lax.axis_index("row")
    col = lax.axis_index("col")
    half = pairs // 2
    own = row // 2 + half * (row % 2)

    def owner(pair):
        return 2 * (pair % half) + pair // half

    def partner(step):
        stride = (step * step * step + 5 * step + 6) // 6
        return col + stride * (1 - 2 * ((col // stride) % 2))

    barrier = pltpu.get_barrier_semaphore()
    for shift in range(1, pairs):
        pl.semaphore_signal(barrier, inc=1, device_id=((row + shift) % pairs, col), device_id_type=MESH)
    for step in range(STEPS):
        pl.semaphore_signal(barrier, inc=1, device_id=(row, partner(step)), device_id_type=MESH)

    load_first = pltpu.make_async_copy(first_ref, kept, local_sem.at[0])
    load_second = pltpu.make_async_copy(second_ref, came.at[0], local_sem.at[1])
    load_first.start()
    load_second.start()
    load_first.wait()
    load_second.wait()
    pl.semaphore_wait(barrier, pairs - 1 + STEPS)

    def gram_copy(step, pair):
        return pltpu.make_async_remote_copy(
            src_ref=gram_out.at[pair], dst_ref=gram_in.at[step, row], send_sem=gram_sent.at[pair],
            recv_sem=gram_came.at[step, row], device_id=(owner(pair), col), device_id_type=MESH)

    def gram_arrival(step, source):
        return pltpu.make_async_remote_copy(
            src_ref=gram_out.at[source], dst_ref=gram_in.at[step, source], send_sem=gram_sent.at[source],
            recv_sem=gram_came.at[step, source], device_id=(source, col), device_id_type=MESH)

    def turn_copy(step, target):
        return pltpu.make_async_remote_copy(
            src_ref=turn.at[step, own], dst_ref=turn.at[step, own], send_sem=turn_sent.at[target],
            recv_sem=turn_came.at[step, own], device_id=(target, col), device_id_type=MESH)

    def turn_arrival(step, pair):
        return pltpu.make_async_remote_copy(
            src_ref=turn.at[step, pair], dst_ref=turn.at[step, pair], send_sem=turn_sent.at[pair],
            recv_sem=turn_came.at[step, pair], device_id=(owner(pair), col), device_id_type=MESH)

    def block_copy(step, pair):
        return pltpu.make_async_remote_copy(
            src_ref=leaving.at[pair], dst_ref=came.at[step + 1, pair], send_sem=block_sent.at[pair],
            recv_sem=block_came.at[step, pair], device_id=(row, partner(step)), device_id_type=MESH)

    def load_pair(step, pair):
        return split_two(jnp.concatenate([kept[pair], came[step, pair]], 0))

    def phase(index, _):
        split = jnp.minimum(index // 2, 1)
        step = (1 - split) * index + split * (2 + (index - 2) // 2)
        start = split * half * (index % 2)
        count = pairs - split * half
        mine = (own >= start) & (own < start + count)

        def gram_one(pair, _):
            @pl.when(step > 0)
            def _():
                block_copy(step - 1, pair).wait_recv()

            high, low = load_pair(step, pair)
            gram = lax.dot_general(
                jnp.concatenate([low, high, high], 1), jnp.concatenate([high, low, high], 1),
                (((1,), (1,)), ((), ())), preferred_element_type=F32)

            @pl.when(pair == own)
            def _():
                pack_gram(gram, gram_in.at[step, row])

            @pl.when(pair != own)
            def _():
                pack_gram(gram, gram_out.at[pair])
                gram_copy(step, pair).start()

            return 0

        lax.fori_loop(start, start + count, gram_one, 0)

        @pl.when(mine)
        def _():
            def arrive(shift, _):
                gram_arrival(step, (row + shift) % pairs).wait_recv()
                return 0

            lax.fori_loop(1, pairs, arrive, 0)
            total = gram_in[step, 0]
            for source in range(1, pairs):
                total = total + gram_in[step, source]
            gram = unpack_gram(total)
            came_first = (step > 0) & (slot_ref[jnp.maximum(step - 1, 0), own] == 0)
            gram = jnp.where(came_first, swap_columns(swap_rows(gram)), gram)
            rotate(gram, a_ref, e_ref, 32)
            turned = e_ref[:, :W]
            turned = jnp.where(came_first, swap_columns(turned), turned)
            turned = jnp.where(slot_ref[step, own] == 0, swap_rows(turned), turned)
            packed = turn.at[step, own]
            packed[0:W, :] = turned[:, 0:128]
            packed[W:, :] = jnp.concatenate([turned[0:BW, 128:W], turned[BW:W, 128:W]], 1)

            def send(shift, _):
                turn_copy(step, (row + shift) % pairs).start()
                return 0

            lax.fori_loop(1, pairs, send, 0)

        def update_one(pair, _):
            @pl.when(pair != own)
            def _():
                turn_arrival(step, pair).wait_recv()
                gram_copy(step, pair).wait_send()

            @pl.when(step > 0)
            def _():
                block_copy(step - 1, pair).wait_send()

            packed = turn[step, pair]
            tail = packed[W:, :]
            turned = jnp.concatenate(
                [packed[0:W, :], jnp.concatenate([tail[:, 0:64], tail[:, 64:128]], 0)], 1)
            turn_high, turn_low = split_two(turned)
            high, low = load_pair(step, pair)
            dims = (((1,), (0,)), ((), ()))
            new = (
                lax.dot_general(turn_low, high, dims, preferred_element_type=F32)
                + lax.dot_general(turn_high, low, dims, preferred_element_type=F32)
                + lax.dot_general(turn_high, high, dims, preferred_element_type=F32))
            kept[pair] = new[0:BW]
            leaving[pair] = new[BW:]
            block_copy(step, pair).start()
            return 0

        lax.fori_loop(start, start + count, update_one, 0)

        @pl.when(mine)
        def _():
            def sent(shift, _):
                turn_copy(step, (row + shift) % pairs).wait_send()
                return 0

            lax.fori_loop(1, pairs, sent, 0)

        return 0

    lax.fori_loop(0, 6, phase, 0)

    store_kept = pltpu.make_async_copy(kept, kept_out, local_sem.at[0])
    store_kept.start()

    def finish(pair, _):
        block_copy(STEPS - 1, pair).wait()
        return 0

    lax.fori_loop(0, pairs, finish, 0)
    store_came = pltpu.make_async_copy(came.at[STEPS], came_out, local_sem.at[1])
    store_came.start()
    store_kept.wait()
    store_came.wait()


def pair_steps(send_slot, first, second):
    pairs, width, rows = first.shape
    block = jax.ShapeDtypeStruct(first.shape, F32)
    dma = pltpu.SemaphoreType.DMA
    return pl.pallas_call(
        functools.partial(pair_kernel, pairs),
        out_shape=[block, block],
        in_specs=[
            pl.BlockSpec(memory_space=pltpu.SMEM),
            pl.BlockSpec(memory_space=pl.ANY),
            pl.BlockSpec(memory_space=pl.ANY),
        ],
        out_specs=[pl.BlockSpec(memory_space=pl.ANY)] * 2,
        scratch_shapes=[
            pltpu.VMEM((pairs, width, rows), F32),
            pltpu.VMEM((STEPS + 1, pairs, width, rows), F32),
            pltpu.VMEM((pairs, width, rows), F32),
            pltpu.VMEM((pairs, 256, 128), F32),
            pltpu.VMEM((STEPS, pairs, 256, 128), F32),
            pltpu.VMEM((STEPS, pairs, 288, 128), F32),
            pltpu.VMEM((W, 256), F32),
            pltpu.VMEM((W, 256), F32),
            dma((pairs,)),
            dma((STEPS, pairs)),
            dma((pairs,)),
            dma((STEPS, pairs)),
            dma((pairs,)),
            dma((STEPS, pairs)),
            dma((2,)),
        ],
        compiler_params=pltpu.CompilerParams(
            collective_id=0, has_side_effects=True, vmem_limit_bytes=VMEM_LIMIT),
        name="pair_steps",
    )(send_slot, first, second)


def gather_kernel(order_ref, hessian_ref, first_ref, second_ref, turned):
    chunk = hessian_ref.shape[0]
    for part in range(hessian_ref.shape[1] // 384):
        turned[4 * part : 4 * part + 4] = jnp.transpose(
            hessian_ref[:, 384 * part : 384 * part + 384]).reshape(4, BW, chunk)
    for pair in range(first_ref.shape[0]):
        first_ref[pair] = turned[order_ref[0, 2 * pair]]
        second_ref[pair] = turned[order_ref[0, 2 * pair + 1]]


def gathered(hessian, block_order):
    rows, columns = hessian.shape
    blocks = columns // BW
    chunk = 256
    shape = jax.ShapeDtypeStruct((blocks // 2, BW, rows), F32)
    spec = pl.BlockSpec((blocks // 2, BW, chunk), lambda i: (0, 0, i))
    return pl.pallas_call(
        gather_kernel,
        grid=(rows // chunk,),
        out_shape=[shape, shape],
        in_specs=[
            pl.BlockSpec(memory_space=pltpu.SMEM),
            pl.BlockSpec((chunk, columns), lambda i: (i, 0)),
        ],
        out_specs=[spec, spec],
        scratch_shapes=[pltpu.VMEM((blocks, BW, chunk), F32)],
        compiler_params=pltpu.CompilerParams(vmem_limit_bytes=VMEM_LIMIT),
        name="gathered",
    )(block_order, hessian)


def scatter_kernel(slot_ref, kept_ref, came_ref, out_ref):
    for pair in range(0, kept_ref.shape[0], 2):
        parts = []
        for each in (pair, pair + 1):
            came_first = slot_ref[STEPS - 1, each] == 0
            kept, came = kept_ref[each], came_ref[each]
            parts += [jnp.where(came_first, came, kept), jnp.where(came_first, kept, came)]
        out_ref[:, 192 * pair : 192 * pair + 384] = jnp.transpose(jnp.concatenate(parts, 0))


def scattered(send_slot, kept, came):
    pairs, width, rows = kept.shape
    chunk = 256
    spec = pl.BlockSpec((pairs, width, chunk), lambda i: (0, 0, i))
    return pl.pallas_call(
        scatter_kernel,
        grid=(rows // chunk,),
        out_shape=jax.ShapeDtypeStruct((rows, pairs * 2 * width), F32),
        in_specs=[pl.BlockSpec(memory_space=pltpu.SMEM), spec, spec],
        out_specs=pl.BlockSpec((chunk, pairs * 2 * width), lambda i: (i, 0)),
        compiler_params=pltpu.CompilerParams(vmem_limit_bytes=VMEM_LIMIT),
        name="scattered",
    )(send_slot, kept, came)


def body(hessian, block_order, send_slot):
    first, second = gathered(hessian, block_order)
    kept, came = pair_steps(send_slot, first, second)
    return scattered(send_slot, kept, came)


def solution(mesh):
    in_specs = (P("row", "col"), P("col", None), P(None, "col"))
    out_specs = P("row", "col")
    return jax.shard_map(body, mesh=mesh, in_specs=in_specs, out_specs=out_specs, check_vma=False)
```

```python
import functools

import jax
import jax.numpy as jnp
from jax import lax
from jax.experimental import pallas as pl
from jax.experimental.pallas import tpu as pltpu
from jax.sharding import PartitionSpec as P

MESH = pl.DeviceIdType.MESH
BW = 96
F32=jnp.float32; BF=jnp.bfloat16
W=192
def pieces(x):
    h=x.astype(BF); r=x-h.astype(F32); m=r.astype(BF); l=(r-m.astype(F32)).astype(BF)
    return h,m,l
def outer(left, right):
    a0,a1,a2=pieces(left); b0,b1,b2=pieces(right)
    a=jnp.concatenate([a2,a0,a1,a1,a0,a0],0)
    b=jnp.concatenate([b0,b2,b1,b0,b1,b0],0)
    return lax.dot_general(a,b,(((0,),(0,)),((),())),preferred_element_type=F32)
def rsqrt(d):
    r=lax.rsqrt(d)
    return r*(1.5-0.5*d*r*r)
def recip(d):
    r = pl.reciprocal(d, approx=True)
    return r * (2.0 - d * r)
def eliminate(rows, base, NB):
    diag=rows[0][:,base:base+NB]
    cols=[jnp.broadcast_to(diag[:,c:c+1],(NB,128)) for c in range(NB)]
    idx=lax.broadcasted_iota(jnp.int32,(NB,128),0)
    rows=[[r[:,i:i+128] for i in range(0,r.shape[1],128)] for r in rows]
    scale=jnp.zeros((NB,128),F32)
    for c in range(NB):
        col=cols[c]
        d=jnp.broadcast_to(col[c:c+1],(NB,128))
        m=jnp.where(idx>c,col*recip(d),0.0)
        scale=jnp.where(idx==c,d,scale)
        for q in range(c+1,NB):
            cols[q]=cols[q]-m*jnp.broadcast_to(col[q:q+1],(NB,128))
        for g in rows:
            for i in range(len(g)):
                g[i]=g[i]-m*jnp.broadcast_to(g[i][c:c+1],(NB,128))
    scale=rsqrt(scale)
    return [jnp.concatenate([x*scale for x in g],1) if len(g)>1 else g[0]*scale for g in rows]
def factor(a_ref, e_ref, NB, ready=None):
    for t in range(W//NB):
        j=t*NB
        lo=(j//128)*128
        panel=[a_ref[j:j+NB,lo:]]
        if e_ref is not None: panel.append(e_ref[j:j+NB,:])
        out=eliminate(panel,j-lo,NB)
        u=out[0]
        ri=lax.broadcasted_iota(jnp.int32,u.shape,0)+(j-lo)
        ci=lax.broadcasted_iota(jnp.int32,u.shape,1)
        u=jnp.where(ci>=ri,u,0.0)
        a_ref[j:j+NB,lo:]=u
        if lo: a_ref[j:j+NB,:lo]=jnp.zeros((NB,lo),F32)
        if e_ref is not None: e_ref[j:j+NB,:]=out[1]
        if ready is not None and (j+NB)%BW==0: ready((j+NB)//BW-1)
        rem=W-j-NB
        if rem==0: break
        left=u[:,j+NB-lo:W-lo]
        a_ref[j+NB:W,lo:]=a_ref[j+NB:W,lo:]-outer(left,u)
        if e_ref is not None:
            e_ref[j+NB:W,:]=e_ref[j+NB:W,:]-outer(left,out[1])
def rotate(g, a_ref, e_ref, NB, ready):
    s=jnp.sum(jnp.sum(g*g,axis=0,keepdims=True),axis=1,keepdims=True)
    y=g/jnp.sqrt(s)
    yy=y[:,:W]
    a_ref[:,:W]=lax.dot_general(yy,yy,(((0,),(0,)),((),())),precision=lax.Precision.HIGHEST,preferred_element_type=F32)
    a_ref[:,W:]=jnp.zeros((W,256-W),F32)
    factor(a_ref,None,NB)
    u=a_ref[...]
    e_ref[...]=u
    uu=u[:,:W]
    a_ref[:,:W]=lax.dot_general(uu,uu,(((1,),(1,)),((),())),precision=lax.Precision.HIGHEST,preferred_element_type=F32)
    a_ref[:,W:]=jnp.zeros((W,256-W),F32)
    factor(a_ref,e_ref,NB,ready)
STEPS = 4
ROWS_LOCAL = 1024
VMEM_LIMIT = 60 * 2**20


def split_two(x):
    high = x.astype(BF)
    return high, (x - high.astype(F32)).astype(BF)


def pack_gram(gram, ref):
    ref[0:W, :] = gram[:, 0:128]
    ref[W : W + 64, :] = jnp.concatenate([gram[128:W, 128:W], jnp.zeros((64, 64), F32)], 1)


def unpack_gram(packed):
    right = jnp.concatenate([jnp.transpose(packed[128:W, :]), packed[W : W + 64, 0:64]], 0)
    return jnp.concatenate([packed[0:W, :], right], 1)


def swap_rows(x):
    return jnp.concatenate([x[BW:], x[:BW]], 0)


def swap_columns(x):
    return jnp.concatenate([x[:, BW:], x[:, :BW]], 1)


def pack_half(half, ref):
    ref[0:BW, :] = half[:, 0:128]
    ref[BW:, :] = jnp.concatenate([half[0:48, 128:W], half[48:BW, 128:W]], 1)


def unpack_half(packed):
    tail = packed[BW:, :]
    right = jnp.concatenate([tail[:, 0:64], tail[:, 64:128]], 0)
    return jnp.concatenate([packed[0:BW, :], right], 1)


def pair_kernel(
    pairs, slot_ref, first_ref, second_ref, kept_out, came_out,
    kept, came, leaving, gram_out, gram_in, cross_out, cross_in, diag_out, diag_in, diag_kept, turn,
    g_ref, a_ref, e_ref,
    gram_sent, gram_came, cross_sent, cross_came, diag_sent, diag_came, turn_sent, turn_came,
    block_sent, block_came, local_sem,
):
    row = lax.axis_index("row")
    col = lax.axis_index("col")
    half = pairs // 2
    own = row // 2 + half * (row % 2)

    def owner(pair):
        return 2 * (pair % half) + pair // half

    def partner(step):
        stride = (step * step * step + 5 * step + 6) // 6
        return col + stride * (1 - 2 * ((col // stride) % 2))

    barrier = pltpu.get_barrier_semaphore()
    for shift in range(1, pairs):
        pl.semaphore_signal(barrier, inc=1, device_id=((row + shift) % pairs, col), device_id_type=MESH)
    for step in range(STEPS):
        pl.semaphore_signal(barrier, inc=1, device_id=(row, partner(step)), device_id_type=MESH)

    load_first = pltpu.make_async_copy(first_ref, kept, local_sem.at[0])
    load_second = pltpu.make_async_copy(second_ref, came.at[0], local_sem.at[1])
    load_first.start()
    load_second.start()
    load_first.wait()
    load_second.wait()
    pl.semaphore_wait(barrier, pairs - 1 + STEPS)

    def gram_copy(pair):
        return pltpu.make_async_remote_copy(
            src_ref=gram_out.at[pair], dst_ref=gram_in.at[row], send_sem=gram_sent.at[pair],
            recv_sem=gram_came.at[row], device_id=(owner(pair), col), device_id_type=MESH)

    def gram_arrival(source):
        return pltpu.make_async_remote_copy(
            src_ref=gram_out.at[source], dst_ref=gram_in.at[source], send_sem=gram_sent.at[source],
            recv_sem=gram_came.at[source], device_id=(source, col), device_id_type=MESH)

    def cross_copy(step, pair):
        return pltpu.make_async_remote_copy(
            src_ref=cross_out.at[pair], dst_ref=cross_in.at[step, row], send_sem=cross_sent.at[pair],
            recv_sem=cross_came.at[step, row], device_id=(owner(pair), col), device_id_type=MESH)

    def cross_arrival(step, source):
        return pltpu.make_async_remote_copy(
            src_ref=cross_out.at[source], dst_ref=cross_in.at[step, source], send_sem=cross_sent.at[source],
            recv_sem=cross_came.at[step, source], device_id=(source, col), device_id_type=MESH)

    def diag_copy(step):
        return pltpu.make_async_remote_copy(
            src_ref=diag_out.at[step], dst_ref=diag_in.at[step], send_sem=diag_sent.at[step],
            recv_sem=diag_came.at[step], device_id=(row, partner(step)), device_id_type=MESH)

    def turn_copy(step, part, target):
        return pltpu.make_async_remote_copy(
            src_ref=turn.at[step, own, part], dst_ref=turn.at[step, own, part],
            send_sem=turn_sent.at[part, target], recv_sem=turn_came.at[step, own, part],
            device_id=(target, col), device_id_type=MESH)

    def turn_arrival(step, part, pair):
        return pltpu.make_async_remote_copy(
            src_ref=turn.at[step, pair, part], dst_ref=turn.at[step, pair, part],
            send_sem=turn_sent.at[part, pair], recv_sem=turn_came.at[step, pair, part],
            device_id=(owner(pair), col), device_id_type=MESH)

    def block_copy(step, pair):
        return pltpu.make_async_remote_copy(
            src_ref=leaving.at[pair], dst_ref=came.at[step + 1, pair], send_sem=block_sent.at[pair],
            recv_sem=block_came.at[step, pair], device_id=(row, partner(step)), device_id_type=MESH)

    def others(function):
        def one(shift, _):
            function((row + shift) % pairs)
            return 0

        lax.fori_loop(1, pairs, one, 0)

    def gram_full(pair):
        high, low = split_two(jnp.concatenate([kept[pair], came[0, pair]], 0))
        gram = lax.dot_general(
            jnp.concatenate([low, high, high], 1), jnp.concatenate([high, low, high], 1),
            (((1,), (1,)), ((), ())), preferred_element_type=F32)

        @pl.when(pair == own)
        def _():
            pack_gram(gram, gram_in.at[row])

        @pl.when(pair != own)
        def _():
            pack_gram(gram, gram_out.at[pair])
            gram_copy(pair).start()

    def gram_cross(step, pair):
        block_copy(step - 1, pair).wait_recv()
        high, low = split_two(kept[pair])
        came_high, came_low = split_two(came[step, pair])
        cross = lax.dot_general(
            jnp.concatenate([low, high, high], 1), jnp.concatenate([came_high, came_low, came_high], 1),
            (((1,), (1,)), ((), ())), preferred_element_type=F32)
        cross = jnp.concatenate([cross, jnp.zeros((BW, 128 - BW), F32)], 1)

        @pl.when(pair == own)
        def _():
            cross_in[step, row] = cross

        @pl.when(pair != own)
        def _():
            cross_out[pair] = cross
            cross_copy(step, pair).start()

    def gram_whole():
        others(lambda source: gram_arrival(source).wait_recv())
        total = gram_in[0]
        for source in range(1, pairs):
            total = total + gram_in[source]
        g_ref[:, :W] = unpack_gram(total)

    def gram_joined(step):
        others(lambda source: cross_arrival(step, source).wait_recv())
        diag_copy(step - 1).wait_recv()
        total = cross_in[step, 0]
        for source in range(1, pairs):
            total = total + cross_in[step, source]
        cross = total[:, :BW]
        g_ref[0:BW, :W] = jnp.concatenate([diag_kept[:, :BW], cross], 1)
        g_ref[BW:W, :W] = jnp.concatenate([jnp.transpose(cross), diag_in[step - 1][:, :BW]], 1)

    def own_rotation(step):
        came_first = (step > 0) & (slot_ref[jnp.maximum(step - 1, 0), own] == 0)
        gram = g_ref[:, :W]
        gram = jnp.where(came_first, swap_columns(swap_rows(gram)), gram)

        def ready(part):
            turned = e_ref[BW * part : BW * part + BW, :W]
            high, low = split_two(jnp.where(came_first, swap_columns(turned), turned))
            pack_half(high.astype(F32) + low.astype(F32), turn.at[step, own, part])
            others(lambda target: turn_copy(step, part, target).start())

        rotate(gram, a_ref, e_ref, 32, ready)

    def turned_of(step, pair):
        halves = [unpack_half(turn[step, pair, part]) for part in range(2)]
        sent_first = slot_ref[step, pair] == 0
        return jnp.concatenate(
            [jnp.where(sent_first, halves[1], halves[0]), jnp.where(sent_first, halves[0], halves[1])], 0)

    def own_diagonals(step):
        turned = turned_of(step, own)
        exact = dict(precision=lax.Precision.HIGHEST, preferred_element_type=F32)
        product = lax.dot_general(turned, g_ref[:, :W], (((1,), (0,)), ((), ())), **exact)
        blank = jnp.zeros((BW, 128 - BW), F32)
        nt = (((1,), (1,)), ((), ()))
        stays = lax.dot_general(product[:BW], turned[:BW], nt, **exact)
        leaves = lax.dot_general(product[BW:], turned[BW:], nt, **exact)
        diag_kept[...] = jnp.concatenate([stays, blank], 1)
        diag_out[step] = jnp.concatenate([leaves, blank], 1)
        diag_copy(step).start()

    def update_one(step, pair):
        @pl.when(pair != own)
        def _():
            turn_arrival(step, 0, pair).wait_recv()
            turn_arrival(step, 1, pair).wait_recv()

            @pl.when(step == 0)
            def _():
                gram_copy(pair).wait_send()

            @pl.when(step > 0)
            def _():
                cross_copy(step, pair).wait_send()

        @pl.when(step > 0)
        def _():
            block_copy(step - 1, pair).wait_send()

        turn_high, turn_low = split_two(turned_of(step, pair))
        high, low = split_two(jnp.concatenate([kept[pair], came[step, pair]], 0))
        dims = (((1,), (0,)), ((), ()))
        new = (
            lax.dot_general(turn_low, high, dims, preferred_element_type=F32)
            + lax.dot_general(turn_high, low, dims, preferred_element_type=F32)
            + lax.dot_general(turn_high, high, dims, preferred_element_type=F32))
        kept[pair] = new[0:BW]
        leaving[pair] = new[BW:]
        block_copy(step, pair).start()

    def phase(index, _):
        split = jnp.minimum(index // 2, 1)
        step = (1 - split) * index + split * (2 + (index - 2) // 2)
        start = split * half * (index % 2)
        count = pairs - split * half
        mine = (own >= start) & (own < start + count)

        def gram_one(i, _):
            pair = start + (own + i) % count

            @pl.when(step == 0)
            def _():
                gram_full(pair)

            @pl.when(step > 0)
            def _():
                gram_cross(step, pair)

            return 0

        lax.fori_loop(0, count, gram_one, 0)

        @pl.when(mine)
        def _():
            @pl.when(step == 0)
            def _():
                gram_whole()

            @pl.when(step > 0)
            def _():
                gram_joined(step)

            own_rotation(step)

        def update_next(i, _):
            update_one(step, start + (own + i) % count)
            return 0

        lax.fori_loop(0, count, update_next, 0)

        @pl.when(mine)
        def _():
            @pl.when(step < STEPS - 1)
            def _():
                own_diagonals(step)
                diag_copy(step).wait_send()

            for part in range(2):
                others(lambda target: turn_copy(step, part, target).wait_send())

        return 0

    lax.fori_loop(0, 6, phase, 0)

    store_kept = pltpu.make_async_copy(kept, kept_out, local_sem.at[0])
    store_kept.start()

    def finish(pair, _):
        block_copy(STEPS - 1, pair).wait()
        return 0

    lax.fori_loop(0, pairs, finish, 0)
    store_came = pltpu.make_async_copy(came.at[STEPS], came_out, local_sem.at[1])
    store_came.start()
    store_kept.wait()
    store_came.wait()


def pair_steps(send_slot, first, second):
    pairs, width, rows = first.shape
    block = jax.ShapeDtypeStruct(first.shape, F32)
    dma = pltpu.SemaphoreType.DMA
    return pl.pallas_call(
        functools.partial(pair_kernel, pairs),
        out_shape=[block, block],
        in_specs=[
            pl.BlockSpec(memory_space=pltpu.SMEM),
            pl.BlockSpec(memory_space=pl.ANY),
            pl.BlockSpec(memory_space=pl.ANY),
        ],
        out_specs=[pl.BlockSpec(memory_space=pl.ANY)] * 2,
        scratch_shapes=[
            pltpu.VMEM((pairs, width, rows), F32),
            pltpu.VMEM((STEPS + 1, pairs, width, rows), F32),
            pltpu.VMEM((pairs, width, rows), F32),
            pltpu.VMEM((pairs, 256, 128), F32),
            pltpu.VMEM((pairs, 256, 128), F32),
            pltpu.VMEM((pairs, width, 128), F32),
            pltpu.VMEM((STEPS, pairs, width, 128), F32),
            pltpu.VMEM((STEPS, width, 128), F32),
            pltpu.VMEM((STEPS, width, 128), F32),
            pltpu.VMEM((width, 128), F32),
            pltpu.VMEM((STEPS, pairs, 2, 144, 128), F32),
            pltpu.VMEM((W, 256), F32),
            pltpu.VMEM((W, 256), F32),
            pltpu.VMEM((W, 256), F32),
            dma((pairs,)),
            dma((pairs,)),
            dma((pairs,)),
            dma((STEPS, pairs)),
            dma((STEPS,)),
            dma((STEPS,)),
            dma((2, pairs)),
            dma((STEPS, pairs, 2)),
            dma((pairs,)),
            dma((STEPS, pairs)),
            dma((2,)),
        ],
        compiler_params=pltpu.CompilerParams(
            collective_id=0, has_side_effects=True, vmem_limit_bytes=VMEM_LIMIT),
        name="pair_steps",
    )(send_slot, first, second)


def gather_kernel(order_ref, hessian_ref, first_ref, second_ref, turned):
    chunk = hessian_ref.shape[0]
    for part in range(hessian_ref.shape[1] // 384):
        turned[4 * part : 4 * part + 4] = jnp.transpose(
            hessian_ref[:, 384 * part : 384 * part + 384]).reshape(4, BW, chunk)
    for pair in range(first_ref.shape[0]):
        first_ref[pair] = turned[order_ref[0, 2 * pair]]
        second_ref[pair] = turned[order_ref[0, 2 * pair + 1]]


def gathered(hessian, block_order):
    rows, columns = hessian.shape
    blocks = columns // BW
    chunk = 256
    shape = jax.ShapeDtypeStruct((blocks // 2, BW, rows), F32)
    spec = pl.BlockSpec((blocks // 2, BW, chunk), lambda i: (0, 0, i))
    return pl.pallas_call(
        gather_kernel,
        grid=(rows // chunk,),
        out_shape=[shape, shape],
        in_specs=[
            pl.BlockSpec(memory_space=pltpu.SMEM),
            pl.BlockSpec((chunk, columns), lambda i: (i, 0)),
        ],
        out_specs=[spec, spec],
        scratch_shapes=[pltpu.VMEM((blocks, BW, chunk), F32)],
        compiler_params=pltpu.CompilerParams(vmem_limit_bytes=VMEM_LIMIT),
        name="gathered",
    )(block_order, hessian)


def scatter_kernel(slot_ref, kept_ref, came_ref, out_ref):
    for pair in range(0, kept_ref.shape[0], 2):
        parts = []
        for each in (pair, pair + 1):
            came_first = slot_ref[STEPS - 1, each] == 0
            kept, came = kept_ref[each], came_ref[each]
            parts += [jnp.where(came_first, came, kept), jnp.where(came_first, kept, came)]
        out_ref[:, 192 * pair : 192 * pair + 384] = jnp.transpose(jnp.concatenate(parts, 0))


def scattered(send_slot, kept, came):
    pairs, width, rows = kept.shape
    chunk = 256
    spec = pl.BlockSpec((pairs, width, chunk), lambda i: (0, 0, i))
    return pl.pallas_call(
        scatter_kernel,
        grid=(rows // chunk,),
        out_shape=jax.ShapeDtypeStruct((rows, pairs * 2 * width), F32),
        in_specs=[pl.BlockSpec(memory_space=pltpu.SMEM), spec, spec],
        out_specs=pl.BlockSpec((chunk, pairs * 2 * width), lambda i: (i, 0)),
        compiler_params=pltpu.CompilerParams(vmem_limit_bytes=VMEM_LIMIT),
        name="scattered",
    )(send_slot, kept, came)


def body(hessian, block_order, send_slot):
    first, second = gathered(hessian, block_order)
    kept, came = pair_steps(send_slot, first, second)
    return scattered(send_slot, kept, came)


def solution(mesh):
    in_specs = (P("row", "col"), P("col", None), P(None, "col"))
    out_specs = P("row", "col")
    return jax.shard_map(body, mesh=mesh, in_specs=in_specs, out_specs=out_specs, check_vma=False)
```

```python
import functools

import jax
import jax.numpy as jnp
from jax import lax
from jax.experimental import pallas as pl
from jax.experimental.pallas import tpu as pltpu
from jax.sharding import PartitionSpec as P

MESH = pl.DeviceIdType.MESH
BW = 96
F32=jnp.float32; BF=jnp.bfloat16
W=192
def pieces(x):
    h=x.astype(BF); r=x-h.astype(F32); m=r.astype(BF); l=(r-m.astype(F32)).astype(BF)
    return h,m,l
def outer(left, right):
    a0,a1,a2=pieces(left); b0,b1,b2=pieces(right)
    a=jnp.concatenate([a2,a0,a1,a1,a0,a0],0)
    b=jnp.concatenate([b0,b2,b1,b0,b1,b0],0)
    return lax.dot_general(a,b,(((0,),(0,)),((),())),preferred_element_type=F32)
def rsqrt(d):
    r=lax.rsqrt(d)
    return r*(1.5-0.5*d*r*r)
def recip(d):
    r = pl.reciprocal(d, approx=True)
    return r * (2.0 - d * r)
def eliminate(rows, base, NB):
    diag=rows[0][:,base:base+NB]
    cols=[jnp.broadcast_to(diag[:,c:c+1],(NB,128)) for c in range(NB)]
    idx=lax.broadcasted_iota(jnp.int32,(NB,128),0)
    rows=[[r[:,i:i+128] for i in range(0,r.shape[1],128)] for r in rows]
    scale=jnp.zeros((NB,128),F32)
    for c in range(NB):
        col=cols[c]
        d=jnp.broadcast_to(col[c:c+1],(NB,128))
        m=jnp.where(idx>c,col*recip(d),0.0)
        scale=jnp.where(idx==c,d,scale)
        for q in range(c+1,NB):
            cols[q]=cols[q]-m*jnp.broadcast_to(col[q:q+1],(NB,128))
        for g in rows:
            for i in range(len(g)):
                g[i]=g[i]-m*jnp.broadcast_to(g[i][c:c+1],(NB,128))
    scale=rsqrt(scale)
    return [jnp.concatenate([x*scale for x in g],1) if len(g)>1 else g[0]*scale for g in rows]
def factor(a_ref, e_ref, NB, ready=None):
    for t in range(W//NB):
        j=t*NB
        lo=(j//128)*128
        panel=[a_ref[j:j+NB,lo:]]
        if e_ref is not None: panel.append(e_ref[j:j+NB,:])
        out=eliminate(panel,j-lo,NB)
        u=out[0]
        ri=lax.broadcasted_iota(jnp.int32,u.shape,0)+(j-lo)
        ci=lax.broadcasted_iota(jnp.int32,u.shape,1)
        u=jnp.where(ci>=ri,u,0.0)
        a_ref[j:j+NB,lo:]=u
        if lo: a_ref[j:j+NB,:lo]=jnp.zeros((NB,lo),F32)
        if e_ref is not None: e_ref[j:j+NB,:]=out[1]
        if ready is not None and (j+NB)%BW==0: ready((j+NB)//BW-1)
        rem=W-j-NB
        if rem==0: break
        left=u[:,j+NB-lo:W-lo]
        a_ref[j+NB:W,lo:]=a_ref[j+NB:W,lo:]-outer(left,u)
        if e_ref is not None:
            e_ref[j+NB:W,:]=e_ref[j+NB:W,:]-outer(left,out[1])
def rotate(g, a_ref, e_ref, NB, ready):
    s=jnp.sum(jnp.sum(g*g,axis=0,keepdims=True),axis=1,keepdims=True)
    y=g/jnp.sqrt(s)
    yy=y[:,:W]
    a_ref[:,:W]=lax.dot_general(yy,yy,(((0,),(0,)),((),())),precision=lax.Precision.HIGHEST,preferred_element_type=F32)
    a_ref[:,W:]=jnp.zeros((W,256-W),F32)
    factor(a_ref,None,NB)
    u=a_ref[...]
    e_ref[...]=u
    uu=u[:,:W]
    a_ref[:,:W]=lax.dot_general(uu,uu,(((1,),(1,)),((),())),precision=lax.Precision.HIGHEST,preferred_element_type=F32)
    a_ref[:,W:]=jnp.zeros((W,256-W),F32)
    factor(a_ref,e_ref,NB,ready)
STEPS = 4
ROWS_LOCAL = 1024
VMEM_LIMIT = 60 * 2**20


def split_two(x):
    high = x.astype(BF)
    return high, (x - high.astype(F32)).astype(BF)


def pack_gram(gram, ref):
    ref[0:W, :] = gram[:, 0:128]
    ref[W : W + 64, :] = jnp.concatenate([gram[128:W, 128:W], jnp.zeros((64, 64), F32)], 1)


def unpack_gram(packed):
    right = jnp.concatenate([jnp.transpose(packed[128:W, :]), packed[W : W + 64, 0:64]], 0)
    return jnp.concatenate([packed[0:W, :], right], 1)


def swap_rows(x):
    return jnp.concatenate([x[BW:], x[:BW]], 0)


def swap_columns(x):
    return jnp.concatenate([x[:, BW:], x[:, :BW]], 1)


def pack_half(half, ref):
    ref[0:BW, :] = half[:, 0:128]
    ref[BW:, :] = jnp.concatenate([half[0:48, 128:W], half[48:BW, 128:W]], 1)


def unpack_half(packed):
    tail = packed[BW:, :]
    right = jnp.concatenate([tail[:, 0:64], tail[:, 64:128]], 0)
    return jnp.concatenate([packed[0:BW, :], right], 1)


def pair_kernel(
    pairs, slot_ref, first_ref, second_ref, kept_out, came_out,
    kept, came, leaving, gram_out, gram_in, cross_out, cross_in, diag_out, diag_in, diag_kept, turn,
    g_ref, a_ref, e_ref,
    gram_sent, gram_came, cross_sent, cross_came, diag_sent, diag_came, turn_sent, turn_came,
    block_sent, block_came, local_sem,
):
    row = lax.axis_index("row")
    col = lax.axis_index("col")
    half = pairs // 2
    own = row // 2 + half * (row % 2)

    def owner(pair):
        return 2 * (pair % half) + pair // half

    def ordered(start, i):
        return start + half * (i // half) + (row // 2 + half - i % half) % half

    def partner(step):
        stride = (step * step * step + 5 * step + 6) // 6
        return col + stride * (1 - 2 * ((col // stride) % 2))

    barrier = pltpu.get_barrier_semaphore()
    for shift in range(1, pairs):
        pl.semaphore_signal(barrier, inc=1, device_id=((row + shift) % pairs, col), device_id_type=MESH)
    for step in range(STEPS):
        pl.semaphore_signal(barrier, inc=1, device_id=(row, partner(step)), device_id_type=MESH)

    load_first = pltpu.make_async_copy(first_ref, kept, local_sem.at[0])
    load_second = pltpu.make_async_copy(second_ref, came.at[0], local_sem.at[1])
    load_first.start()
    load_second.start()
    load_first.wait()
    load_second.wait()
    pl.semaphore_wait(barrier, pairs - 1 + STEPS)

    def gram_copy(pair):
        return pltpu.make_async_remote_copy(
            src_ref=gram_out.at[pair], dst_ref=gram_in.at[row], send_sem=gram_sent.at[pair],
            recv_sem=gram_came.at[row], device_id=(owner(pair), col), device_id_type=MESH)

    def gram_arrival(source):
        return pltpu.make_async_remote_copy(
            src_ref=gram_out.at[source], dst_ref=gram_in.at[source], send_sem=gram_sent.at[source],
            recv_sem=gram_came.at[source], device_id=(source, col), device_id_type=MESH)

    def cross_copy(step, pair):
        return pltpu.make_async_remote_copy(
            src_ref=cross_out.at[pair], dst_ref=cross_in.at[step, row], send_sem=cross_sent.at[pair],
            recv_sem=cross_came.at[step, row], device_id=(owner(pair), col), device_id_type=MESH)

    def cross_arrival(step, source):
        return pltpu.make_async_remote_copy(
            src_ref=cross_out.at[source], dst_ref=cross_in.at[step, source], send_sem=cross_sent.at[source],
            recv_sem=cross_came.at[step, source], device_id=(source, col), device_id_type=MESH)

    def diag_copy(step):
        return pltpu.make_async_remote_copy(
            src_ref=diag_out.at[step], dst_ref=diag_in.at[step], send_sem=diag_sent.at[step],
            recv_sem=diag_came.at[step], device_id=(row, partner(step)), device_id_type=MESH)

    def turn_copy(step, part, target):
        return pltpu.make_async_remote_copy(
            src_ref=turn.at[step, own, part], dst_ref=turn.at[step, own, part],
            send_sem=turn_sent.at[part, target], recv_sem=turn_came.at[step, own, part],
            device_id=(target, col), device_id_type=MESH)

    def turn_arrival(step, part, pair):
        return pltpu.make_async_remote_copy(
            src_ref=turn.at[step, pair, part], dst_ref=turn.at[step, pair, part],
            send_sem=turn_sent.at[part, pair], recv_sem=turn_came.at[step, pair, part],
            device_id=(owner(pair), col), device_id_type=MESH)

    def block_copy(step, pair):
        return pltpu.make_async_remote_copy(
            src_ref=leaving.at[pair], dst_ref=came.at[step + 1, pair], send_sem=block_sent.at[pair],
            recv_sem=block_came.at[step, pair], device_id=(row, partner(step)), device_id_type=MESH)

    def others(function):
        def one(shift, _):
            function((row + shift) % pairs)
            return 0

        lax.fori_loop(1, pairs, one, 0)

    def gram_full(pair):
        high, low = split_two(jnp.concatenate([kept[pair], came[0, pair]], 0))
        gram = lax.dot_general(
            jnp.concatenate([low, high, high], 1), jnp.concatenate([high, low, high], 1),
            (((1,), (1,)), ((), ())), preferred_element_type=F32)

        @pl.when(pair == own)
        def _():
            pack_gram(gram, gram_in.at[row])

        @pl.when(pair != own)
        def _():
            pack_gram(gram, gram_out.at[pair])
            gram_copy(pair).start()

    def gram_cross(step, pair):
        block_copy(step - 1, pair).wait_recv()
        high, low = split_two(kept[pair])
        came_high, came_low = split_two(came[step, pair])
        cross = lax.dot_general(
            jnp.concatenate([low, high, high], 1), jnp.concatenate([came_high, came_low, came_high], 1),
            (((1,), (1,)), ((), ())), preferred_element_type=F32)
        cross = jnp.concatenate([cross, jnp.zeros((BW, 128 - BW), F32)], 1)

        @pl.when(pair == own)
        def _():
            cross_in[step, row] = cross

        @pl.when(pair != own)
        def _():
            cross_out[pair] = cross
            cross_copy(step, pair).start()

    def gram_whole():
        others(lambda source: gram_arrival(source).wait_recv())
        total = gram_in[0]
        for source in range(1, pairs):
            total = total + gram_in[source]
        g_ref[:, :W] = unpack_gram(total)

    def gram_joined(step):
        others(lambda source: cross_arrival(step, source).wait_recv())
        diag_copy(step - 1).wait_recv()
        total = cross_in[step, 0]
        for source in range(1, pairs):
            total = total + cross_in[step, source]
        cross = total[:, :BW]
        g_ref[0:BW, :W] = jnp.concatenate([diag_kept[:, :BW], cross], 1)
        g_ref[BW:W, :W] = jnp.concatenate([jnp.transpose(cross), diag_in[step - 1][:, :BW]], 1)

    def own_rotation(step):
        came_first = (step > 0) & (slot_ref[jnp.maximum(step - 1, 0), own] == 0)
        gram = g_ref[:, :W]
        gram = jnp.where(came_first, swap_columns(swap_rows(gram)), gram)

        def ready(part):
            turned = e_ref[BW * part : BW * part + BW, :W]
            high, low = split_two(jnp.where(came_first, swap_columns(turned), turned))
            pack_half(high.astype(F32) + low.astype(F32), turn.at[step, own, part])
            others(lambda target: turn_copy(step, part, target).start())

        rotate(gram, a_ref, e_ref, 32, ready)

    def turned_of(step, pair):
        halves = [unpack_half(turn[step, pair, part]) for part in range(2)]
        sent_first = slot_ref[step, pair] == 0
        return jnp.concatenate(
            [jnp.where(sent_first, halves[1], halves[0]), jnp.where(sent_first, halves[0], halves[1])], 0)

    def own_diagonals(step):
        turned = turned_of(step, own)
        exact = dict(precision=lax.Precision.HIGHEST, preferred_element_type=F32)
        product = lax.dot_general(turned, g_ref[:, :W], (((1,), (0,)), ((), ())), **exact)
        blank = jnp.zeros((BW, 128 - BW), F32)
        nt = (((1,), (1,)), ((), ()))
        stays = lax.dot_general(product[:BW], turned[:BW], nt, **exact)
        leaves = lax.dot_general(product[BW:], turned[BW:], nt, **exact)
        diag_kept[...] = jnp.concatenate([stays, blank], 1)
        diag_out[step] = jnp.concatenate([leaves, blank], 1)
        diag_copy(step).start()

    def update_one(step, pair):
        @pl.when(pair != own)
        def _():
            turn_arrival(step, 0, pair).wait_recv()
            turn_arrival(step, 1, pair).wait_recv()

            @pl.when(step == 0)
            def _():
                gram_copy(pair).wait_send()

            @pl.when(step > 0)
            def _():
                cross_copy(step, pair).wait_send()

        @pl.when(step > 0)
        def _():
            block_copy(step - 1, pair).wait_send()

        turn_high, turn_low = split_two(turned_of(step, pair))
        high, low = split_two(jnp.concatenate([kept[pair], came[step, pair]], 0))
        dims = (((1,), (0,)), ((), ()))
        new = (
            lax.dot_general(turn_low, high, dims, preferred_element_type=F32)
            + lax.dot_general(turn_high, low, dims, preferred_element_type=F32)
            + lax.dot_general(turn_high, high, dims, preferred_element_type=F32))
        kept[pair] = new[0:BW]
        leaving[pair] = new[BW:]
        block_copy(step, pair).start()

    def phase(index, _):
        split = jnp.minimum(index // 2, 1)
        step = (1 - split) * index + split * (2 + (index - 2) // 2)
        start = split * half * (index % 2)
        count = pairs - split * half
        mine = (own >= start) & (own < start + count)

        def gram_one(i, _):
            pair = ordered(start, i)

            @pl.when(step == 0)
            def _():
                gram_full(pair)

            @pl.when(step > 0)
            def _():
                gram_cross(step, pair)

            return 0

        lax.fori_loop(0, count, gram_one, 0)

        @pl.when(mine)
        def _():
            @pl.when(step == 0)
            def _():
                gram_whole()

            @pl.when(step > 0)
            def _():
                gram_joined(step)

            own_rotation(step)

        def update_next(i, _):
            update_one(step, ordered(start, i))
            return 0

        lax.fori_loop(0, count, update_next, 0)

        @pl.when(mine)
        def _():
            @pl.when(step < STEPS - 1)
            def _():
                own_diagonals(step)
                diag_copy(step).wait_send()

            for part in range(2):
                others(lambda target: turn_copy(step, part, target).wait_send())

        return 0

    lax.fori_loop(0, 6, phase, 0)

    store_kept = pltpu.make_async_copy(kept, kept_out, local_sem.at[0])
    store_kept.start()

    def finish(pair, _):
        block_copy(STEPS - 1, pair).wait()
        return 0

    lax.fori_loop(0, pairs, finish, 0)
    store_came = pltpu.make_async_copy(came.at[STEPS], came_out, local_sem.at[1])
    store_came.start()
    store_kept.wait()
    store_came.wait()


def pair_steps(send_slot, first, second):
    pairs, width, rows = first.shape
    block = jax.ShapeDtypeStruct(first.shape, F32)
    dma = pltpu.SemaphoreType.DMA
    return pl.pallas_call(
        functools.partial(pair_kernel, pairs),
        out_shape=[block, block],
        in_specs=[
            pl.BlockSpec(memory_space=pltpu.SMEM),
            pl.BlockSpec(memory_space=pl.ANY),
            pl.BlockSpec(memory_space=pl.ANY),
        ],
        out_specs=[pl.BlockSpec(memory_space=pl.ANY)] * 2,
        scratch_shapes=[
            pltpu.VMEM((pairs, width, rows), F32),
            pltpu.VMEM((STEPS + 1, pairs, width, rows), F32),
            pltpu.VMEM((pairs, width, rows), F32),
            pltpu.VMEM((pairs, 256, 128), F32),
            pltpu.VMEM((pairs, 256, 128), F32),
            pltpu.VMEM((pairs, width, 128), F32),
            pltpu.VMEM((STEPS, pairs, width, 128), F32),
            pltpu.VMEM((STEPS, width, 128), F32),
            pltpu.VMEM((STEPS, width, 128), F32),
            pltpu.VMEM((width, 128), F32),
            pltpu.VMEM((STEPS, pairs, 2, 144, 128), F32),
            pltpu.VMEM((W, 256), F32),
            pltpu.VMEM((W, 256), F32),
            pltpu.VMEM((W, 256), F32),
            dma((pairs,)),
            dma((pairs,)),
            dma((pairs,)),
            dma((STEPS, pairs)),
            dma((STEPS,)),
            dma((STEPS,)),
            dma((2, pairs)),
            dma((STEPS, pairs, 2)),
            dma((pairs,)),
            dma((STEPS, pairs)),
            dma((2,)),
        ],
        compiler_params=pltpu.CompilerParams(
            collective_id=0, has_side_effects=True, vmem_limit_bytes=VMEM_LIMIT),
        name="pair_steps",
    )(send_slot, first, second)


def gather_kernel(order_ref, hessian_ref, first_ref, second_ref, turned):
    chunk = hessian_ref.shape[0]
    for part in range(hessian_ref.shape[1] // 384):
        turned[4 * part : 4 * part + 4] = jnp.transpose(
            hessian_ref[:, 384 * part : 384 * part + 384]).reshape(4, BW, chunk)
    for pair in range(first_ref.shape[0]):
        first_ref[pair] = turned[order_ref[0, 2 * pair]]
        second_ref[pair] = turned[order_ref[0, 2 * pair + 1]]


def gathered(hessian, block_order):
    rows, columns = hessian.shape
    blocks = columns // BW
    chunk = 256
    shape = jax.ShapeDtypeStruct((blocks // 2, BW, rows), F32)
    spec = pl.BlockSpec((blocks // 2, BW, chunk), lambda i: (0, 0, i))
    return pl.pallas_call(
        gather_kernel,
        grid=(rows // chunk,),
        out_shape=[shape, shape],
        in_specs=[
            pl.BlockSpec(memory_space=pltpu.SMEM),
            pl.BlockSpec((chunk, columns), lambda i: (i, 0)),
        ],
        out_specs=[spec, spec],
        scratch_shapes=[pltpu.VMEM((blocks, BW, chunk), F32)],
        compiler_params=pltpu.CompilerParams(vmem_limit_bytes=VMEM_LIMIT),
        name="gathered",
    )(block_order, hessian)


def scatter_kernel(slot_ref, kept_ref, came_ref, out_ref):
    for pair in range(0, kept_ref.shape[0], 2):
        parts = []
        for each in (pair, pair + 1):
            came_first = slot_ref[STEPS - 1, each] == 0
            kept, came = kept_ref[each], came_ref[each]
            parts += [jnp.where(came_first, came, kept), jnp.where(came_first, kept, came)]
        out_ref[:, 192 * pair : 192 * pair + 384] = jnp.transpose(jnp.concatenate(parts, 0))


def scattered(send_slot, kept, came):
    pairs, width, rows = kept.shape
    chunk = 256
    spec = pl.BlockSpec((pairs, width, chunk), lambda i: (0, 0, i))
    return pl.pallas_call(
        scatter_kernel,
        grid=(rows // chunk,),
        out_shape=jax.ShapeDtypeStruct((rows, pairs * 2 * width), F32),
        in_specs=[pl.BlockSpec(memory_space=pltpu.SMEM), spec, spec],
        out_specs=pl.BlockSpec((chunk, pairs * 2 * width), lambda i: (i, 0)),
        compiler_params=pltpu.CompilerParams(vmem_limit_bytes=VMEM_LIMIT),
        name="scattered",
    )(send_slot, kept, came)


def body(hessian, block_order, send_slot):
    first, second = gathered(hessian, block_order)
    kept, came = pair_steps(send_slot, first, second)
    return scattered(send_slot, kept, came)


def solution(mesh):
    in_specs = (P("row", "col"), P("col", None), P(None, "col"))
    out_specs = P("row", "col")
    return jax.shard_map(body, mesh=mesh, in_specs=in_specs, out_specs=out_specs, check_vma=False)
```

```python
import functools

import jax
import jax.numpy as jnp
from jax import lax
from jax.experimental import pallas as pl
from jax.experimental.pallas import tpu as pltpu
from jax.sharding import PartitionSpec as P

MESH = pl.DeviceIdType.MESH
BW = 96
F32=jnp.float32; BF=jnp.bfloat16
W=192;BW=96
def pieces(x):
    h=x.astype(BF); r=x-h.astype(F32); m=r.astype(BF); l=(r-m.astype(F32)).astype(BF)
    return h,m,l
def outer(left, right):
    a0,a1,a2=pieces(left); b0,b1,b2=pieces(right)
    a=jnp.concatenate([a2,a0,a1,a1,a0,a0],0)
    b=jnp.concatenate([b0,b2,b1,b0,b1,b0],0)
    return lax.dot_general(a,b,(((0,),(0,)),((),())),preferred_element_type=F32)
def rsqrt(d):
    r=lax.rsqrt(d)
    return r*(1.5-0.5*d*r*r)
def recip(d):
    r = pl.reciprocal(d, approx=True)
    return r * (2.0 - d * r)
def eliminate(rows, base, NB):
    diag=rows[0][:,base:base+NB]
    cols=[jnp.broadcast_to(diag[:,c:c+1],(NB,128)) for c in range(NB)]
    idx=lax.broadcasted_iota(jnp.int32,(NB,128),0)
    rows=[[r[:,i:i+128] for i in range(0,r.shape[1],128)] for r in rows]
    scale=jnp.zeros((NB,128),F32)
    for c in range(NB):
        col=cols[c]
        d=jnp.broadcast_to(col[c:c+1],(NB,128))
        m=jnp.where(idx>c,col*recip(d),0.0)
        scale=jnp.where(idx==c,d,scale)
        for q in range(c+1,NB):
            cols[q]=cols[q]-m*jnp.broadcast_to(col[q:q+1],(NB,128))
        for g in rows:
            for i in range(len(g)):
                g[i]=g[i]-m*jnp.broadcast_to(g[i][c:c+1],(NB,128))
    scale=rsqrt(scale)
    return [jnp.concatenate([x*scale for x in g],1) if len(g)>1 else g[0]*scale for g in rows]
def factor(a_ref, e_ref, NB, ready=None):
    for t in range(W//NB):
        j=t*NB
        lo=(j//128)*128
        panel=[a_ref[j:j+NB,lo:]]
        if e_ref is not None: panel.append(e_ref[j:j+NB,:])
        out=eliminate(panel,j-lo,NB)
        u=out[0]
        ri=lax.broadcasted_iota(jnp.int32,u.shape,0)+(j-lo)
        ci=lax.broadcasted_iota(jnp.int32,u.shape,1)
        u=jnp.where(ci>=ri,u,0.0)
        a_ref[j:j+NB,lo:]=u
        if lo: a_ref[j:j+NB,:lo]=jnp.zeros((NB,lo),F32)
        if e_ref is not None: e_ref[j:j+NB,:]=out[1]
        if ready is not None and (j+NB)%BW==0: ready((j+NB)//BW-1)
        rem=W-j-NB
        if rem==0: break
        left=u[:,j+NB-lo:W-lo]
        a_ref[j+NB:W,lo:]=a_ref[j+NB:W,lo:]-outer(left,u)
        if e_ref is not None:
            e_ref[j+NB:W,:]=e_ref[j+NB:W,:]-outer(left,out[1])
def rotate(g, a_ref, e_ref, NB, ready):
    s=jnp.sum(jnp.sum(g*g,axis=0,keepdims=True),axis=1,keepdims=True)
    y=g/jnp.sqrt(s)
    yy=y[:,:W]
    a_ref[:,:W]=lax.dot_general(yy,yy,(((0,),(0,)),((),())),precision=lax.Precision.HIGHEST,preferred_element_type=F32)
    a_ref[:,W:]=jnp.zeros((W,256-W),F32)
    factor(a_ref,None,NB)
    u=a_ref[...]
    e_ref[...]=u
    uu=u[:,:W]
    a_ref[:,:W]=lax.dot_general(uu,uu,(((1,),(1,)),((),())),precision=lax.Precision.HIGHEST,preferred_element_type=F32)
    a_ref[:,W:]=jnp.zeros((W,256-W),F32)
    factor(a_ref,e_ref,NB,ready)
STEPS = 4
ROWS_LOCAL = 1024
VMEM_LIMIT = 60 * 2**20


def split_two(x):
    high = x.astype(BF)
    return high, (x - high.astype(F32)).astype(BF)


def pack_gram(gram, ref):
    ref[0:W, :] = gram[:, 0:128]
    ref[W : W + 64, :] = jnp.concatenate([gram[128:W, 128:W], jnp.zeros((64, 64), F32)], 1)


def unpack_gram(packed):
    right = jnp.concatenate([jnp.transpose(packed[128:W, :]), packed[W : W + 64, 0:64]], 0)
    return jnp.concatenate([packed[0:W, :], right], 1)


def swap_rows(x):
    return jnp.concatenate([x[BW:], x[:BW]], 0)


def swap_columns(x):
    return jnp.concatenate([x[:, BW:], x[:, :BW]], 1)


def pack_half(half, ref):
    ref[0:BW, :] = half[:, 0:128]
    ref[BW:, :] = jnp.concatenate([half[0:48, 128:W], half[48:BW, 128:W]], 1)


def unpack_half(packed):
    tail = packed[BW:, :]
    right = jnp.concatenate([tail[:, 0:64], tail[:, 64:128]], 0)
    return jnp.concatenate([packed[0:BW, :], right], 1)


def pair_kernel(
    pairs, slot_ref, first_ref, second_ref, kept_out, came_out,
    kept, came, leaving, gram_out, gram_in, cross_out, cross_in, diag_out, diag_in, diag_kept, turn,
    g_ref, a_ref, e_ref,
    gram_sent, gram_came, cross_sent, cross_came, diag_sent, diag_came, turn_sent, turn_came,
    block_sent, block_came, local_sem,
):
    row = lax.axis_index("row")
    col = lax.axis_index("col")
    half = pairs // 2
    across = (row + half) % pairs
    plane = row // half * half
    own = row // 2 + half * (row % 2)
    beyond = across // 2 + half * (across % 2)

    def owner(pair):
        return 2 * (pair % half) + pair // half

    def ordered(start, i):
        return start + half * (i // half) + (row // 2 + half - i % half) % half

    def partner(step):
        stride = (step * step * step + 5 * step + 6) // 6
        return col + stride * (1 - 2 * ((col // stride) % 2))

    barrier = pltpu.get_barrier_semaphore()
    for shift in range(1, pairs):
        pl.semaphore_signal(barrier, inc=1, device_id=((row + shift) % pairs, col), device_id_type=MESH)
    for step in range(STEPS):
        pl.semaphore_signal(barrier, inc=1, device_id=(row, partner(step)), device_id_type=MESH)

    load_first = pltpu.make_async_copy(first_ref, kept, local_sem.at[0])
    load_second = pltpu.make_async_copy(second_ref, came.at[0], local_sem.at[1])
    load_first.start()
    load_second.start()
    load_first.wait()
    load_second.wait()
    pl.semaphore_wait(barrier, pairs - 1 + STEPS)

    def gram_copy(pair):
        return pltpu.make_async_remote_copy(
            src_ref=gram_out.at[pair], dst_ref=gram_in.at[row], send_sem=gram_sent.at[pair],
            recv_sem=gram_came.at[row], device_id=(owner(pair), col), device_id_type=MESH)

    def gram_arrival(source):
        return pltpu.make_async_remote_copy(
            src_ref=gram_out.at[source], dst_ref=gram_in.at[source], send_sem=gram_sent.at[source],
            recv_sem=gram_came.at[source], device_id=(source, col), device_id_type=MESH)

    def cross_copy(step, pair):
        return pltpu.make_async_remote_copy(
            src_ref=cross_out.at[pair], dst_ref=cross_in.at[step, row], send_sem=cross_sent.at[pair],
            recv_sem=cross_came.at[step, row], device_id=(owner(pair), col), device_id_type=MESH)

    def cross_arrival(step, source):
        return pltpu.make_async_remote_copy(
            src_ref=cross_out.at[source], dst_ref=cross_in.at[step, source], send_sem=cross_sent.at[source],
            recv_sem=cross_came.at[step, source], device_id=(source, col), device_id_type=MESH)

    def diag_copy(step):
        return pltpu.make_async_remote_copy(
            src_ref=diag_out.at[step], dst_ref=diag_in.at[step], send_sem=diag_sent.at[step],
            recv_sem=diag_came.at[step], device_id=(row, partner(step)), device_id_type=MESH)

    def turn_copy(step, part, pair, target):
        return pltpu.make_async_remote_copy(
            src_ref=turn.at[step, pair, part], dst_ref=turn.at[step, pair, part],
            send_sem=turn_sent.at[part, pair // 2 % 2, target], recv_sem=turn_came.at[step, pair, part],
            device_id=(target, col), device_id_type=MESH)

    def turn_arrival(step, part, pair):
        return pltpu.make_async_remote_copy(
            src_ref=turn.at[step, pair, part], dst_ref=turn.at[step, pair, part],
            send_sem=turn_sent.at[part, 0, 0], recv_sem=turn_came.at[step, pair, part],
            device_id=(across, col), device_id_type=MESH)

    def block_copy(step, pair):
        return pltpu.make_async_remote_copy(
            src_ref=leaving.at[pair], dst_ref=came.at[step + 1, pair], send_sem=block_sent.at[pair],
            recv_sem=block_came.at[step, pair], device_id=(row, partner(step)), device_id_type=MESH)

    def others(function):
        def one(shift, _):
            function((row + shift) % pairs)
            return 0

        lax.fori_loop(1, pairs, one, 0)

    def neighbours(function):
        def one(shift, _):
            function(plane + (row - plane + shift) % half)
            return 0

        lax.fori_loop(1, half, one, 0)

    def gram_full(pair):
        high, low = split_two(jnp.concatenate([kept[pair], came[0, pair]], 0))
        gram = lax.dot_general(
            jnp.concatenate([low, high, high], 1), jnp.concatenate([high, low, high], 1),
            (((1,), (1,)), ((), ())), preferred_element_type=F32)

        @pl.when(pair == own)
        def _():
            pack_gram(gram, gram_in.at[row])

        @pl.when(pair != own)
        def _():
            pack_gram(gram, gram_out.at[pair])
            gram_copy(pair).start()

    def gram_cross(step, pair):
        block_copy(step - 1, pair).wait_recv()
        high, low = split_two(kept[pair])
        came_high, came_low = split_two(came[step, pair])
        cross = lax.dot_general(
            jnp.concatenate([low, high, high], 1), jnp.concatenate([came_high, came_low, came_high], 1),
            (((1,), (1,)), ((), ())), preferred_element_type=F32)
        cross = jnp.concatenate([cross, jnp.zeros((BW, 128 - BW), F32)], 1)

        @pl.when(pair == own)
        def _():
            cross_in[step, row] = cross

        @pl.when(pair != own)
        def _():
            cross_out[pair] = cross
            cross_copy(step, pair).start()

    def gram_whole():
        others(lambda source: gram_arrival(source).wait_recv())
        total = gram_in[0]
        for source in range(1, pairs):
            total = total + gram_in[source]
        g_ref[:, :W] = unpack_gram(total)

    def gram_joined(step):
        others(lambda source: cross_arrival(step, source).wait_recv())
        diag_copy(step - 1).wait_recv()
        total = cross_in[step, 0]
        for source in range(1, pairs):
            total = total + cross_in[step, source]
        cross = total[:, :BW]
        g_ref[0:BW, :W] = jnp.concatenate([diag_kept[:, :BW], cross], 1)
        g_ref[BW:W, :W] = jnp.concatenate([jnp.transpose(cross), diag_in[step - 1][:, :BW]], 1)

    def own_rotation(step):
        came_first = (step > 0) & (slot_ref[jnp.maximum(step - 1, 0), own] == 0)
        gram = g_ref[:, :W]
        gram = jnp.where(came_first, swap_columns(swap_rows(gram)), gram)

        def ready(part):
            turned = e_ref[BW * part : BW * part + BW, :W]
            high, low = split_two(jnp.where(came_first, swap_columns(turned), turned))
            pack_half(high.astype(F32) + low.astype(F32), turn.at[step, own, part])
            turn_copy(step, part, own, across).start()
            neighbours(lambda target: turn_copy(step, part, own, target).start())

        rotate(gram, a_ref, e_ref, 32, ready)

    def turned_of(step, pair):
        halves = [unpack_half(turn[step, pair, part]) for part in range(2)]
        sent_first = slot_ref[step, pair] == 0
        return jnp.concatenate(
            [jnp.where(sent_first, halves[1], halves[0]), jnp.where(sent_first, halves[0], halves[1])], 0)

    def own_diagonals(step):
        turned = turned_of(step, own)
        exact = dict(precision=lax.Precision.HIGHEST, preferred_element_type=F32)
        product = lax.dot_general(turned, g_ref[:, :W], (((1,), (0,)), ((), ())), **exact)
        blank = jnp.zeros((BW, 128 - BW), F32)
        nt = (((1,), (1,)), ((), ()))
        stays = lax.dot_general(product[:BW], turned[:BW], nt, **exact)
        leaves = lax.dot_general(product[BW:], turned[BW:], nt, **exact)
        diag_kept[...] = jnp.concatenate([stays, blank], 1)
        diag_out[step] = jnp.concatenate([leaves, blank], 1)
        diag_copy(step).start()

    def update_one(step, pair):
        @pl.when((pair != own) & (pair != beyond))
        def _():
            turn_arrival(step, 0, pair).wait_recv()
            turn_arrival(step, 1, pair).wait_recv()

        @pl.when(pair != own)
        def _():
            @pl.when(step == 0)
            def _():
                gram_copy(pair).wait_send()

            @pl.when(step > 0)
            def _():
                cross_copy(step, pair).wait_send()

        @pl.when(step > 0)
        def _():
            block_copy(step - 1, pair).wait_send()

        turn_high, turn_low = split_two(turned_of(step, pair))
        high, low = split_two(jnp.concatenate([kept[pair], came[step, pair]], 0))
        dims = (((1,), (0,)), ((), ()))
        new = (
            lax.dot_general(turn_low, high, dims, preferred_element_type=F32)
            + lax.dot_general(turn_high, low, dims, preferred_element_type=F32)
            + lax.dot_general(turn_high, high, dims, preferred_element_type=F32))
        kept[pair] = new[0:BW]
        leaving[pair] = new[BW:]
        block_copy(step, pair).start()

    def phase(index, _):
        split = jnp.minimum(index // 2, 1)
        step = (1 - split) * index + split * (2 + (index - 2) // 2)
        start = split * half * (index % 2)
        count = pairs - split * half
        mine = (own >= start) & (own < start + count)

        def gram_one(i, _):
            pair = ordered(start, i)

            @pl.when(step == 0)
            def _():
                gram_full(pair)

            @pl.when(step > 0)
            def _():
                gram_cross(step, pair)

            return 0

        lax.fori_loop(0, count, gram_one, 0)

        @pl.when(mine)
        def _():
            @pl.when(step == 0)
            def _():
                gram_whole()

            @pl.when(step > 0)
            def _():
                gram_joined(step)

            own_rotation(step)
            for part in range(2):
                turn_arrival(step, part, beyond).wait_recv()
                neighbours(lambda target: turn_copy(step, part, beyond, target).start())

        def update_next(i, _):
            update_one(step, ordered(start, i))
            return 0

        lax.fori_loop(0, count, update_next, 0)

        @pl.when(mine)
        def _():
            @pl.when(step < STEPS - 1)
            def _():
                own_diagonals(step)
                diag_copy(step).wait_send()

            for part in range(2):
                turn_copy(step, part, own, across).wait_send()
                neighbours(lambda target: turn_copy(step, part, own, target).wait_send())
                neighbours(lambda target: turn_copy(step, part, beyond, target).wait_send())

        return 0

    lax.fori_loop(0, 6, phase, 0)

    store_kept = pltpu.make_async_copy(kept, kept_out, local_sem.at[0])
    store_kept.start()

    def finish(pair, _):
        block_copy(STEPS - 1, pair).wait()
        return 0

    lax.fori_loop(0, pairs, finish, 0)
    store_came = pltpu.make_async_copy(came.at[STEPS], came_out, local_sem.at[1])
    store_came.start()
    store_kept.wait()
    store_came.wait()


def pair_steps(send_slot, first, second):
    pairs, width, rows = first.shape
    block = jax.ShapeDtypeStruct(first.shape, F32)
    dma = pltpu.SemaphoreType.DMA
    return pl.pallas_call(
        functools.partial(pair_kernel, pairs),
        out_shape=[block, block],
        in_specs=[
            pl.BlockSpec(memory_space=pltpu.SMEM),
            pl.BlockSpec(memory_space=pl.ANY),
            pl.BlockSpec(memory_space=pl.ANY),
        ],
        out_specs=[pl.BlockSpec(memory_space=pl.ANY)] * 2,
        scratch_shapes=[
            pltpu.VMEM((pairs, width, rows), F32),
            pltpu.VMEM((STEPS + 1, pairs, width, rows), F32),
            pltpu.VMEM((pairs, width, rows), F32),
            pltpu.VMEM((pairs, 256, 128), F32),
            pltpu.VMEM((pairs, 256, 128), F32),
            pltpu.VMEM((pairs, width, 128), F32),
            pltpu.VMEM((STEPS, pairs, width, 128), F32),
            pltpu.VMEM((STEPS, width, 128), F32),
            pltpu.VMEM((STEPS, width, 128), F32),
            pltpu.VMEM((width, 128), F32),
            pltpu.VMEM((STEPS, pairs, 2, 144, 128), F32),
            pltpu.VMEM((W, 256), F32),
            pltpu.VMEM((W, 256), F32),
            pltpu.VMEM((W, 256), F32),
            dma((pairs,)),
            dma((pairs,)),
            dma((pairs,)),
            dma((STEPS, pairs)),
            dma((STEPS,)),
            dma((STEPS,)),
            dma((2, 2, pairs)),
            dma((STEPS, pairs, 2)),
            dma((pairs,)),
            dma((STEPS, pairs)),
            dma((2,)),
        ],
        compiler_params=pltpu.CompilerParams(
            collective_id=0, has_side_effects=True, vmem_limit_bytes=VMEM_LIMIT),
        name="pair_steps",
    )(send_slot, first, second)


def gather_kernel(order_ref, hessian_ref, first_ref, second_ref, turned):
    chunk = hessian_ref.shape[0]
    for part in range(hessian_ref.shape[1] // 384):
        turned[4 * part : 4 * part + 4] = jnp.transpose(
            hessian_ref[:, 384 * part : 384 * part + 384]).reshape(4, BW, chunk)
    for pair in range(first_ref.shape[0]):
        first_ref[pair] = turned[order_ref[0, 2 * pair]]
        second_ref[pair] = turned[order_ref[0, 2 * pair + 1]]


def gathered(hessian, block_order):
    rows, columns = hessian.shape
    blocks = columns // BW
    chunk = 256
    shape = jax.ShapeDtypeStruct((blocks // 2, BW, rows), F32)
    spec = pl.BlockSpec((blocks // 2, BW, chunk), lambda i: (0, 0, i))
    return pl.pallas_call(
        gather_kernel,
        grid=(rows // chunk,),
        out_shape=[shape, shape],
        in_specs=[
            pl.BlockSpec(memory_space=pltpu.SMEM),
            pl.BlockSpec((chunk, columns), lambda i: (i, 0)),
        ],
        out_specs=[spec, spec],
        scratch_shapes=[pltpu.VMEM((blocks, BW, chunk), F32)],
        compiler_params=pltpu.CompilerParams(vmem_limit_bytes=VMEM_LIMIT),
        name="gathered",
    )(block_order, hessian)


def scatter_kernel(slot_ref, kept_ref, came_ref, out_ref):
    for pair in range(0, kept_ref.shape[0], 2):
        parts = []
        for each in (pair, pair + 1):
            came_first = slot_ref[STEPS - 1, each] == 0
            kept, came = kept_ref[each], came_ref[each]
            parts += [jnp.where(came_first, came, kept), jnp.where(came_first, kept, came)]
        out_ref[:, 192 * pair : 192 * pair + 384] = jnp.transpose(jnp.concatenate(parts, 0))


def scattered(send_slot, kept, came):
    pairs, width, rows = kept.shape
    chunk = 256
    spec = pl.BlockSpec((pairs, width, chunk), lambda i: (0, 0, i))
    return pl.pallas_call(
        scatter_kernel,
        grid=(rows // chunk,),
        out_shape=jax.ShapeDtypeStruct((rows, pairs * 2 * width), F32),
        in_specs=[pl.BlockSpec(memory_space=pltpu.SMEM), spec, spec],
        out_specs=pl.BlockSpec((chunk, pairs * 2 * width), lambda i: (i, 0)),
        compiler_params=pltpu.CompilerParams(vmem_limit_bytes=VMEM_LIMIT),
        name="scattered",
    )(send_slot, kept, came)


def body(hessian, block_order, send_slot):
    first, second = gathered(hessian, block_order)
    kept, came = pair_steps(send_slot, first, second)
    return scattered(send_slot, kept, came)


def solution(mesh):
    in_specs = (P("row", "col"), P("col", None), P(None, "col"))
    out_specs = P("row", "col")
    return jax.shard_map(body, mesh=mesh, in_specs=in_specs, out_specs=out_specs, check_vma=False)
```

```python
import functools

import jax
import jax.numpy as jnp
from jax import lax
from jax.experimental import pallas as pl
from jax.experimental.pallas import tpu as pltpu
from jax.sharding import PartitionSpec as P

MESH = pl.DeviceIdType.MESH
BW = 96
F32=jnp.float32; BF=jnp.bfloat16
W=192;BW=96
def pieces(x):
    h=x.astype(BF); r=x-h.astype(F32); m=r.astype(BF); l=(r-m.astype(F32)).astype(BF)
    return h,m,l
def outer(left, right):
    a0,a1,a2=pieces(left); b0,b1,b2=pieces(right)
    a=jnp.concatenate([a2,a0,a1,a1,a0,a0],0)
    b=jnp.concatenate([b0,b2,b1,b0,b1,b0],0)
    return lax.dot_general(a,b,(((0,),(0,)),((),())),preferred_element_type=F32)
def rsqrt(d):
    r=lax.rsqrt(d)
    return r*(1.5-0.5*d*r*r)
def recip(d):
    r = pl.reciprocal(d, approx=True)
    return r * (2.0 - d * r)
def eliminate(rows, base, NB):
    diag=rows[0][:,base:base+NB]
    cols=[jnp.broadcast_to(diag[:,c:c+1],(NB,128)) for c in range(NB)]
    idx=lax.broadcasted_iota(jnp.int32,(NB,128),0)
    rows=[[r[:,i:i+128] for i in range(0,r.shape[1],128)] for r in rows]
    scale=jnp.zeros((NB,128),F32)
    for c in range(NB):
        col=cols[c]
        d=jnp.broadcast_to(col[c:c+1],(NB,128))
        m=jnp.where(idx>c,col*recip(d),0.0)
        scale=jnp.where(idx==c,d,scale)
        for q in range(c+1,NB):
            cols[q]=cols[q]-m*jnp.broadcast_to(col[q:q+1],(NB,128))
        for g in rows:
            for i in range(len(g)):
                g[i]=g[i]-m*jnp.broadcast_to(g[i][c:c+1],(NB,128))
    scale=rsqrt(scale)
    return [jnp.concatenate([x*scale for x in g],1) if len(g)>1 else g[0]*scale for g in rows]
def factor(a_ref, e_ref, NB, ready=None):
    for t in range(W//NB):
        j=t*NB
        lo=(j//128)*128
        panel=[a_ref[j:j+NB,lo:]]
        if e_ref is not None: panel.append(e_ref[j:j+NB,:])
        out=eliminate(panel,j-lo,NB)
        u=out[0]
        ri=lax.broadcasted_iota(jnp.int32,u.shape,0)+(j-lo)
        ci=lax.broadcasted_iota(jnp.int32,u.shape,1)
        u=jnp.where(ci>=ri,u,0.0)
        a_ref[j:j+NB,lo:]=u
        if lo: a_ref[j:j+NB,:lo]=jnp.zeros((NB,lo),F32)
        if e_ref is not None: e_ref[j:j+NB,:]=out[1]
        if ready is not None and (j+NB)%BW==0: ready((j+NB)//BW-1)
        rem=W-j-NB
        if rem==0: break
        left=u[:,j+NB-lo:W-lo]
        a_ref[j+NB:W,lo:]=a_ref[j+NB:W,lo:]-outer(left,u)
        if e_ref is not None:
            e_ref[j+NB:W,:]=e_ref[j+NB:W,:]-outer(left,out[1])
def rotate(g, a_ref, e_ref, NB, ready):
    s=jnp.sum(jnp.sum(g*g,axis=0,keepdims=True),axis=1,keepdims=True)
    y=g/jnp.sqrt(s)
    yy=y[:,:W]
    a_ref[:,:W]=lax.dot_general(yy,yy,(((0,),(0,)),((),())),precision=lax.Precision.HIGHEST,preferred_element_type=F32)
    a_ref[:,W:]=jnp.zeros((W,256-W),F32)
    factor(a_ref,None,NB)
    u=a_ref[...]
    e_ref[...]=u
    uu=u[:,:W]
    a_ref[:,:W]=lax.dot_general(uu,uu,(((1,),(1,)),((),())),precision=lax.Precision.HIGHEST,preferred_element_type=F32)
    a_ref[:,W:]=jnp.zeros((W,256-W),F32)
    factor(a_ref,e_ref,NB,ready)
STEPS = 4
ROWS_LOCAL = 1024
VMEM_LIMIT = 60 * 2**20


def split_two(x):
    high = x.astype(BF)
    return high, (x - high.astype(F32)).astype(BF)


def pack_gram(gram, ref):
    ref[0:W, :] = gram[:, 0:128]
    ref[W : W + 64, :] = jnp.concatenate([gram[128:W, 128:W], jnp.zeros((64, 64), F32)], 1)


def unpack_gram(packed):
    right = jnp.concatenate([jnp.transpose(packed[128:W, :]), packed[W : W + 64, 0:64]], 0)
    return jnp.concatenate([packed[0:W, :], right], 1)


def swap_rows(x):
    return jnp.concatenate([x[BW:], x[:BW]], 0)


def swap_columns(x):
    return jnp.concatenate([x[:, BW:], x[:, :BW]], 1)


def pack_half(half, ref):
    ref[0:BW, :] = half[:, 0:128]
    ref[BW:, :] = jnp.concatenate([half[0:48, 128:W], half[48:BW, 128:W]], 1)


def unpack_half(packed):
    tail = packed[BW:, :]
    right = jnp.concatenate([tail[:, 0:64], tail[:, 64:128]], 0)
    return jnp.concatenate([packed[0:BW, :], right], 1)


def pair_kernel(
    pairs, slot_ref, first_ref, second_ref, kept_out, came_out,
    kept, came, leaving, gram_out, gram_in, cross_out, cross_in, diag_out, diag_in, diag_kept, turn,
    g_ref, a_ref, e_ref,
    gram_sent, gram_came, cross_sent, cross_came, diag_sent, diag_came, turn_sent, turn_came,
    block_sent, block_came, local_sem,
):
    row = lax.axis_index("row")
    col = lax.axis_index("col")
    half = pairs // 2
    across = (row + half) % pairs
    plane = row // half * half
    own = row // 2 + half * (row % 2)
    beyond = across // 2 + half * (across % 2)

    def owner(pair):
        return 2 * (pair % half) + pair // half

    def ordered(start, i):
        return start + half * (i // half) + (row // 2 + half - i % half) % half

    def partner(step):
        stride = (step * step * step + 5 * step + 6) // 6
        return col + stride * (1 - 2 * ((col // stride) % 2))

    barrier = pltpu.get_barrier_semaphore()
    for shift in range(1, pairs):
        pl.semaphore_signal(barrier, inc=1, device_id=((row + shift) % pairs, col), device_id_type=MESH)
    for step in range(STEPS):
        pl.semaphore_signal(barrier, inc=1, device_id=(row, partner(step)), device_id_type=MESH)

    load_first = pltpu.make_async_copy(first_ref, kept, local_sem.at[0])
    load_second = pltpu.make_async_copy(second_ref, came.at[0], local_sem.at[1])
    load_first.start()
    load_second.start()
    load_first.wait()
    load_second.wait()
    pl.semaphore_wait(barrier, pairs - 1 + STEPS)

    def gram_copy(pair):
        return pltpu.make_async_remote_copy(
            src_ref=gram_out.at[pair], dst_ref=gram_in.at[row], send_sem=gram_sent.at[pair],
            recv_sem=gram_came.at[row], device_id=(owner(pair), col), device_id_type=MESH)

    def gram_arrival(source):
        return pltpu.make_async_remote_copy(
            src_ref=gram_out.at[source], dst_ref=gram_in.at[source], send_sem=gram_sent.at[source],
            recv_sem=gram_came.at[source], device_id=(source, col), device_id_type=MESH)

    def cross_copy(step, pair):
        return pltpu.make_async_remote_copy(
            src_ref=cross_out.at[pair], dst_ref=cross_in.at[step, row], send_sem=cross_sent.at[pair],
            recv_sem=cross_came.at[step, row], device_id=(owner(pair), col), device_id_type=MESH)

    def cross_arrival(step, source):
        return pltpu.make_async_remote_copy(
            src_ref=cross_out.at[source], dst_ref=cross_in.at[step, source], send_sem=cross_sent.at[source],
            recv_sem=cross_came.at[step, source], device_id=(source, col), device_id_type=MESH)

    def diag_copy(step):
        return pltpu.make_async_remote_copy(
            src_ref=diag_out.at[step], dst_ref=diag_in.at[step], send_sem=diag_sent.at[step],
            recv_sem=diag_came.at[step], device_id=(row, partner(step)), device_id_type=MESH)

    def turn_copy(step, part, pair, target):
        return pltpu.make_async_remote_copy(
            src_ref=turn.at[step, pair, part], dst_ref=turn.at[step, pair, part],
            send_sem=turn_sent.at[part, pair // 2 % 2, target], recv_sem=turn_came.at[step, pair, part],
            device_id=(target, col), device_id_type=MESH)

    def turn_arrival(step, part, pair):
        return pltpu.make_async_remote_copy(
            src_ref=turn.at[step, pair, part], dst_ref=turn.at[step, pair, part],
            send_sem=turn_sent.at[part, 0, 0], recv_sem=turn_came.at[step, pair, part],
            device_id=(across, col), device_id_type=MESH)

    def block_copy(step, pair):
        return pltpu.make_async_remote_copy(
            src_ref=leaving.at[pair], dst_ref=came.at[step + 1, pair], send_sem=block_sent.at[pair],
            recv_sem=block_came.at[step, pair], device_id=(row, partner(step)), device_id_type=MESH)

    def others(function):
        def one(shift, _):
            function((row + shift) % pairs)
            return 0

        lax.fori_loop(1, pairs, one, 0)

    def neighbours(function):
        def one(shift, _):
            function(plane + (row - plane + shift) % half)
            return 0

        lax.fori_loop(1, half, one, 0)

    def gram_full(pair):
        high, low = split_two(jnp.concatenate([kept[pair], came[0, pair]], 0))
        gram = lax.dot_general(
            jnp.concatenate([low, high, high], 1), jnp.concatenate([high, low, high], 1),
            (((1,), (1,)), ((), ())), preferred_element_type=F32)

        @pl.when(pair == own)
        def _():
            pack_gram(gram, gram_in.at[row])

        @pl.when(pair != own)
        def _():
            pack_gram(gram, gram_out.at[pair])
            gram_copy(pair).start()

    def gram_cross(step, pair):
        block_copy(step - 1, pair).wait_recv()
        high, low = split_two(kept[pair])
        came_high, came_low = split_two(came[step, pair])
        cross = lax.dot_general(
            jnp.concatenate([low, high, high], 1), jnp.concatenate([came_high, came_low, came_high], 1),
            (((1,), (1,)), ((), ())), preferred_element_type=F32)
        cross = jnp.concatenate([cross, jnp.zeros((BW, 128 - BW), F32)], 1)

        @pl.when(pair == own)
        def _():
            cross_in[step, row] = cross

        @pl.when(pair != own)
        def _():
            cross_out[pair] = cross
            cross_copy(step, pair).start()

    def gram_whole():
        others(lambda source: gram_arrival(source).wait_recv())
        total = gram_in[0]
        for source in range(1, pairs):
            total = total + gram_in[source]
        g_ref[:, :W] = unpack_gram(total)

    def gram_joined(step):
        others(lambda source: cross_arrival(step, source).wait_recv())
        diag_copy(step - 1).wait_recv()
        total = cross_in[step, 0]
        for source in range(1, pairs):
            total = total + cross_in[step, source]
        cross = total[:, :BW]
        g_ref[0:BW, :W] = jnp.concatenate([diag_kept[:, :BW], cross], 1)
        g_ref[BW:W, :W] = jnp.concatenate([jnp.transpose(cross), diag_in[step - 1][:, :BW]], 1)

    def own_rotation(step):
        came_first = (step > 0) & (slot_ref[jnp.maximum(step - 1, 0), own] == 0)
        gram = g_ref[:, :W]
        gram = jnp.where(came_first, swap_columns(swap_rows(gram)), gram)

        def ready(part):
            turned = e_ref[BW * part : BW * part + BW, :W]
            high, low = split_two(jnp.where(came_first, swap_columns(turned), turned))
            pack_half(high.astype(F32) + low.astype(F32), turn.at[step, own, part])
            turn_copy(step, part, own, across).start()
            neighbours(lambda target: turn_copy(step, part, own, target).start())

        rotate(gram, a_ref, e_ref, 32, ready)

    def turned_of(step, pair):
        halves = [unpack_half(turn[step, pair, part]) for part in range(2)]
        sent_first = slot_ref[step, pair] == 0
        return jnp.concatenate(
            [jnp.where(sent_first, halves[1], halves[0]), jnp.where(sent_first, halves[0], halves[1])], 0)

    def own_diagonals(step):
        turned = turned_of(step, own)
        exact = dict(precision=lax.Precision.HIGHEST, preferred_element_type=F32)
        product = lax.dot_general(turned, g_ref[:, :W], (((1,), (0,)), ((), ())), **exact)
        blank = jnp.zeros((BW, 128 - BW), F32)
        nt = (((1,), (1,)), ((), ()))
        stays = lax.dot_general(product[:BW], turned[:BW], nt, **exact)
        leaves = lax.dot_general(product[BW:], turned[BW:], nt, **exact)
        diag_kept[...] = jnp.concatenate([stays, blank], 1)
        diag_out[step] = jnp.concatenate([leaves, blank], 1)
        diag_copy(step).start()

    def update_one(step, pair):
        @pl.when((pair != own) & (pair != beyond))
        def _():
            turn_arrival(step, 0, pair).wait_recv()
            turn_arrival(step, 1, pair).wait_recv()

        @pl.when(pair != own)
        def _():
            @pl.when(step == 0)
            def _():
                gram_copy(pair).wait_send()

            @pl.when(step > 0)
            def _():
                cross_copy(step, pair).wait_send()

        @pl.when(step > 0)
        def _():
            block_copy(step - 1, pair).wait_send()

        turn_high, turn_low = split_two(turned_of(step, pair))
        high, low = split_two(jnp.concatenate([kept[pair], came[step, pair]], 0))
        dims = (((1,), (0,)), ((), ()))
        new = (
            lax.dot_general(turn_low, high, dims, preferred_element_type=F32)
            + lax.dot_general(turn_high, low, dims, preferred_element_type=F32)
            + lax.dot_general(turn_high, high, dims, preferred_element_type=F32))
        kept[pair] = new[0:BW]
        leaving[pair] = new[BW:]
        block_copy(step, pair).start()

    def phase(index, _):
        split = jnp.minimum(index // 2, 1)
        step = (1 - split) * index + split * (2 + (index - 2) // 2)
        start = split * half * (index % 2)
        count = pairs - split * half
        mine = (own >= start) & (own < start + count)

        def gram_one(i, _):
            pair = ordered(start, i)

            @pl.when(step == 0)
            def _():
                gram_full(pair)

            @pl.when(step > 0)
            def _():
                gram_cross(step, pair)

            return 0

        lax.fori_loop(0, count, gram_one, 0)

        @pl.when(mine)
        def _():
            @pl.when(step == 0)
            def _():
                gram_whole()

            @pl.when(step > 0)
            def _():
                gram_joined(step)

            own_rotation(step)

            @pl.when(step < STEPS - 1)
            def _():
                own_diagonals(step)

            for part in range(2):
                turn_arrival(step, part, beyond).wait_recv()
                neighbours(lambda target: turn_copy(step, part, beyond, target).start())

        def update_next(i, _):
            update_one(step, ordered(start, i))
            return 0

        lax.fori_loop(0, count, update_next, 0)

        @pl.when(mine)
        def _():
            @pl.when(step < STEPS - 1)
            def _():
                diag_copy(step).wait_send()

            for part in range(2):
                turn_copy(step, part, own, across).wait_send()
                neighbours(lambda target: turn_copy(step, part, own, target).wait_send())
                neighbours(lambda target: turn_copy(step, part, beyond, target).wait_send())

        return 0

    lax.fori_loop(0, 6, phase, 0)

    store_kept = pltpu.make_async_copy(kept, kept_out, local_sem.at[0])
    store_kept.start()

    def finish(pair, _):
        block_copy(STEPS - 1, pair).wait()
        return 0

    lax.fori_loop(0, pairs, finish, 0)
    store_came = pltpu.make_async_copy(came.at[STEPS], came_out, local_sem.at[1])
    store_came.start()
    store_kept.wait()
    store_came.wait()


def pair_steps(send_slot, first, second):
    pairs, width, rows = first.shape
    block = jax.ShapeDtypeStruct(first.shape, F32)
    dma = pltpu.SemaphoreType.DMA
    return pl.pallas_call(
        functools.partial(pair_kernel, pairs),
        out_shape=[block, block],
        in_specs=[
            pl.BlockSpec(memory_space=pltpu.SMEM),
            pl.BlockSpec(memory_space=pl.ANY),
            pl.BlockSpec(memory_space=pl.ANY),
        ],
        out_specs=[pl.BlockSpec(memory_space=pl.ANY)] * 2,
        scratch_shapes=[
            pltpu.VMEM((pairs, width, rows), F32),
            pltpu.VMEM((STEPS + 1, pairs, width, rows), F32),
            pltpu.VMEM((pairs, width, rows), F32),
            pltpu.VMEM((pairs, 256, 128), F32),
            pltpu.VMEM((pairs, 256, 128), F32),
            pltpu.VMEM((pairs, width, 128), F32),
            pltpu.VMEM((STEPS, pairs, width, 128), F32),
            pltpu.VMEM((STEPS, width, 128), F32),
            pltpu.VMEM((STEPS, width, 128), F32),
            pltpu.VMEM((width, 128), F32),
            pltpu.VMEM((STEPS, pairs, 2, 144, 128), F32),
            pltpu.VMEM((W, 256), F32),
            pltpu.VMEM((W, 256), F32),
            pltpu.VMEM((W, 256), F32),
            dma((pairs,)),
            dma((pairs,)),
            dma((pairs,)),
            dma((STEPS, pairs)),
            dma((STEPS,)),
            dma((STEPS,)),
            dma((2, 2, pairs)),
            dma((STEPS, pairs, 2)),
            dma((pairs,)),
            dma((STEPS, pairs)),
            dma((2,)),
        ],
        compiler_params=pltpu.CompilerParams(
            collective_id=0, has_side_effects=True, vmem_limit_bytes=VMEM_LIMIT),
        name="pair_steps",
    )(send_slot, first, second)


def gather_kernel(order_ref, hessian_ref, first_ref, second_ref, turned):
    chunk = hessian_ref.shape[0]
    for part in range(hessian_ref.shape[1] // 384):
        turned[4 * part : 4 * part + 4] = jnp.transpose(
            hessian_ref[:, 384 * part : 384 * part + 384]).reshape(4, BW, chunk)
    for pair in range(first_ref.shape[0]):
        first_ref[pair] = turned[order_ref[0, 2 * pair]]
        second_ref[pair] = turned[order_ref[0, 2 * pair + 1]]


def gathered(hessian, block_order):
    rows, columns = hessian.shape
    blocks = columns // BW
    chunk = 256
    shape = jax.ShapeDtypeStruct((blocks // 2, BW, rows), F32)
    spec = pl.BlockSpec((blocks // 2, BW, chunk), lambda i: (0, 0, i))
    return pl.pallas_call(
        gather_kernel,
        grid=(rows // chunk,),
        out_shape=[shape, shape],
        in_specs=[
            pl.BlockSpec(memory_space=pltpu.SMEM),
            pl.BlockSpec((chunk, columns), lambda i: (i, 0)),
        ],
        out_specs=[spec, spec],
        scratch_shapes=[pltpu.VMEM((blocks, BW, chunk), F32)],
        compiler_params=pltpu.CompilerParams(vmem_limit_bytes=VMEM_LIMIT),
        name="gathered",
    )(block_order, hessian)


def scatter_kernel(slot_ref, kept_ref, came_ref, out_ref):
    for pair in range(0, kept_ref.shape[0], 2):
        parts = []
        for each in (pair, pair + 1):
            came_first = slot_ref[STEPS - 1, each] == 0
            kept, came = kept_ref[each], came_ref[each]
            parts += [jnp.where(came_first, came, kept), jnp.where(came_first, kept, came)]
        out_ref[:, 192 * pair : 192 * pair + 384] = jnp.transpose(jnp.concatenate(parts, 0))


def scattered(send_slot, kept, came):
    pairs, width, rows = kept.shape
    chunk = 256
    spec = pl.BlockSpec((pairs, width, chunk), lambda i: (0, 0, i))
    return pl.pallas_call(
        scatter_kernel,
        grid=(rows // chunk,),
        out_shape=jax.ShapeDtypeStruct((rows, pairs * 2 * width), F32),
        in_specs=[pl.BlockSpec(memory_space=pltpu.SMEM), spec, spec],
        out_specs=pl.BlockSpec((chunk, pairs * 2 * width), lambda i: (i, 0)),
        compiler_params=pltpu.CompilerParams(vmem_limit_bytes=VMEM_LIMIT),
        name="scattered",
    )(send_slot, kept, came)


def body(hessian, block_order, send_slot):
    first, second = gathered(hessian, block_order)
    kept, came = pair_steps(send_slot, first, second)
    return scattered(send_slot, kept, came)


def solution(mesh):
    in_specs = (P("row", "col"), P("col", None), P(None, "col"))
    out_specs = P("row", "col")
    return jax.shard_map(body, mesh=mesh, in_specs=in_specs, out_specs=out_specs, check_vma=False)
```

```python
import functools

import jax
import jax.numpy as jnp
from jax import lax
from jax.experimental import pallas as pl
from jax.experimental.pallas import tpu as pltpu
from jax.sharding import PartitionSpec as P

MESH = pl.DeviceIdType.MESH

F32=jnp.float32; BF=jnp.bfloat16
W=192;BW=96
def pieces(x):
    h=x.astype(BF); r=x-h.astype(F32); m=r.astype(BF); l=(r-m.astype(F32)).astype(BF)
    return h,m,l
def outer(left, right):
    a0,a1,a2=pieces(left); b0,b1,b2=pieces(right)
    a=jnp.concatenate([a2,a0,a1,a1,a0,a0],0)
    b=jnp.concatenate([b0,b2,b1,b0,b1,b0],0)
    return lax.dot_general(a,b,(((0,),(0,)),((),())),preferred_element_type=F32)
def rsqrt(d):
    r=lax.rsqrt(d)
    return r*(1.5-0.5*d*r*r)
def recip(d):
    return 1.0/d
def eliminate(rows, base, NB):
    diag=rows[0][:,base:base+NB]
    cols=[jnp.broadcast_to(diag[:,c:c+1],(NB,128)) for c in range(NB)]
    idx=lax.broadcasted_iota(jnp.int32,(NB,128),0)
    rows=[[r[:,i:i+128] for i in range(0,r.shape[1],128)] for r in rows]
    scale=jnp.zeros((NB,128),F32)
    for c in range(NB):
        col=cols[c]
        d=jnp.broadcast_to(col[c:c+1],(NB,128))
        m=jnp.where(idx>c,col*recip(d),0.0)
        scale=jnp.where(idx==c,d,scale)
        for q in range(c+1,NB):
            cols[q]=cols[q]-m*jnp.broadcast_to(col[q:q+1],(NB,128))
        for g in rows:
            for i in range(len(g)):
                g[i]=g[i]-m*jnp.broadcast_to(g[i][c:c+1],(NB,128))
    scale=rsqrt(scale)
    return [jnp.concatenate([x*scale for x in g],1) if len(g)>1 else g[0]*scale for g in rows]
def factor(a_ref, e_ref, NB, ready=None):
    for t in range(W//NB):
        j=t*NB
        lo=(j//128)*128
        panel=[a_ref[j:j+NB,lo:]]
        if e_ref is not None: panel.append(e_ref[j:j+NB,:])
        out=eliminate(panel,j-lo,NB)
        u=out[0]
        ri=lax.broadcasted_iota(jnp.int32,u.shape,0)+(j-lo)
        ci=lax.broadcasted_iota(jnp.int32,u.shape,1)
        u=jnp.where(ci>=ri,u,0.0)
        a_ref[j:j+NB,lo:]=u
        if lo: a_ref[j:j+NB,:lo]=jnp.zeros((NB,lo),F32)
        if e_ref is not None: e_ref[j:j+NB,:]=out[1]
        if ready is not None and (j+NB)%BW==0: ready((j+NB)//BW-1)
        rem=W-j-NB
        if rem==0: break
        left=u[:,j+NB-lo:W-lo]
        a_ref[j+NB:W,lo:]=a_ref[j+NB:W,lo:]-outer(left,u)
        if e_ref is not None:
            e_ref[j+NB:W,:]=e_ref[j+NB:W,:]-outer(left,out[1])
def rotate(g, a_ref, e_ref, NB, ready):
    s=jnp.sum(jnp.sum(g*g,axis=0,keepdims=True),axis=1,keepdims=True)
    y=g/jnp.sqrt(s)
    yy=y[:,:W]
    a_ref[:,:W]=lax.dot_general(yy,yy,(((0,),(0,)),((),())),precision=lax.Precision.HIGHEST,preferred_element_type=F32)
    a_ref[:,W:]=jnp.zeros((W,256-W),F32)
    factor(a_ref,None,NB)
    u=a_ref[...]
    e_ref[...]=u
    uu=u[:,:W]
    a_ref[:,:W]=lax.dot_general(uu,uu,(((1,),(1,)),((),())),precision=lax.Precision.HIGHEST,preferred_element_type=F32)
    a_ref[:,W:]=jnp.zeros((W,256-W),F32)
    factor(a_ref,e_ref,NB,ready)
STEPS = 4
ROWS_LOCAL = 1024
VMEM_LIMIT = 60 * 2**20


def split_two(x):
    high = x.astype(BF)
    return high, (x - high.astype(F32)).astype(BF)


def pack_gram(gram, ref):
    ref[0:W, :] = gram[:, 0:128]
    ref[W : W + 64, :] = jnp.concatenate([gram[128:W, 128:W], jnp.zeros((64, 64), F32)], 1)


def unpack_gram(packed):
    right = jnp.concatenate([jnp.transpose(packed[128:W, :]), packed[W : W + 64, 0:64]], 0)
    return jnp.concatenate([packed[0:W, :], right], 1)


def swap_rows(x):
    return jnp.concatenate([x[BW:], x[:BW]], 0)


def swap_columns(x):
    return jnp.concatenate([x[:, BW:], x[:, :BW]], 1)


def pack_half(half, ref):
    ref[0:BW, :] = half[:, 0:128]
    ref[BW:, :] = jnp.concatenate([half[0:48, 128:W], half[48:BW, 128:W]], 1)


def unpack_half(packed):
    tail = packed[BW:, :]
    right = jnp.concatenate([tail[:, 0:64], tail[:, 64:128]], 0)
    return jnp.concatenate([packed[0:BW, :], right], 1)


def pair_kernel(
    pairs, slot_ref, order_ref, hessian_ref, kept_out, came_out,
    slab, turned, kept, came, leaving, gram_out, gram_in, cross_out, cross_in, diag_out, diag_in, diag_kept, turn,
    g_ref, a_ref, e_ref,
    gram_sent, gram_came, cross_sent, cross_came, diag_sent, diag_came, turn_sent, turn_came,
    block_sent, block_came, load_sem, local_sem,
):
    row = lax.axis_index("row")
    col = lax.axis_index("col")
    half = pairs // 2
    across = (row + half) % pairs
    plane = row // half * half
    own = row // 2 + half * (row % 2)
    beyond = across // 2 + half * (across % 2)

    def owner(pair):
        return 2 * (pair % half) + pair // half

    def ordered(start, i):
        return start + half * (i // half) + (row // 2 + half - i % half) % half

    def partner(step):
        stride = (step * step * step + 5 * step + 6) // 6
        return col + stride * (1 - 2 * ((col // stride) % 2))

    chunk = turned.shape[2]
    chunks = slab.shape[0] // chunk

    def load(index):
        rows = pl.ds(pl.multiple_of(index * chunk, chunk), chunk)
        return pltpu.make_async_copy(hessian_ref.at[rows], slab.at[rows], load_sem.at[index])

    for index in range(chunks):
        load(index).start()

    barrier = pltpu.get_barrier_semaphore()
    for shift in range(1, pairs):
        pl.semaphore_signal(barrier, inc=1, device_id=((row + shift) % pairs, col), device_id_type=MESH)
    for step in range(STEPS):
        pl.semaphore_signal(barrier, inc=1, device_id=(row, partner(step)), device_id_type=MESH)

    def gather(index, _):
        load(index).wait()
        rows = pl.ds(pl.multiple_of(index * chunk, chunk), chunk)
        for part in range(slab.shape[1] // 384):
            turned[4 * part : 4 * part + 4] = jnp.transpose(
                slab[rows, 384 * part : 384 * part + 384]).reshape(4, BW, chunk)
        for pair in range(pairs):
            kept[pair, :, rows] = turned[order_ref[0, 2 * pair]]
            came[0, pair, :, rows] = turned[order_ref[0, 2 * pair + 1]]
        return 0

    lax.fori_loop(0, chunks, gather, 0)
    pl.semaphore_wait(barrier, pairs - 1 + STEPS)

    def gram_copy(pair):
        return pltpu.make_async_remote_copy(
            src_ref=gram_out.at[pair], dst_ref=gram_in.at[row], send_sem=gram_sent.at[pair],
            recv_sem=gram_came.at[row], device_id=(owner(pair), col), device_id_type=MESH)

    def gram_arrival(source):
        return pltpu.make_async_remote_copy(
            src_ref=gram_out.at[source], dst_ref=gram_in.at[source], send_sem=gram_sent.at[source],
            recv_sem=gram_came.at[source], device_id=(source, col), device_id_type=MESH)

    def cross_copy(step, pair):
        return pltpu.make_async_remote_copy(
            src_ref=cross_out.at[pair], dst_ref=cross_in.at[step, row], send_sem=cross_sent.at[pair],
            recv_sem=cross_came.at[step, row], device_id=(owner(pair), col), device_id_type=MESH)

    def cross_arrival(step, source):
        return pltpu.make_async_remote_copy(
            src_ref=cross_out.at[source], dst_ref=cross_in.at[step, source], send_sem=cross_sent.at[source],
            recv_sem=cross_came.at[step, source], device_id=(source, col), device_id_type=MESH)

    def diag_copy(step):
        return pltpu.make_async_remote_copy(
            src_ref=diag_out.at[step], dst_ref=diag_in.at[step], send_sem=diag_sent.at[step],
            recv_sem=diag_came.at[step], device_id=(row, partner(step)), device_id_type=MESH)

    def turn_copy(step, part, pair, target):
        return pltpu.make_async_remote_copy(
            src_ref=turn.at[step, pair, part], dst_ref=turn.at[step, pair, part],
            send_sem=turn_sent.at[part, pair // 2 % 2, target], recv_sem=turn_came.at[step, pair, part],
            device_id=(target, col), device_id_type=MESH)

    def turn_arrival(step, part, pair):
        return pltpu.make_async_remote_copy(
            src_ref=turn.at[step, pair, part], dst_ref=turn.at[step, pair, part],
            send_sem=turn_sent.at[part, 0, 0], recv_sem=turn_came.at[step, pair, part],
            device_id=(across, col), device_id_type=MESH)

    def block_copy(step, pair):
        return pltpu.make_async_remote_copy(
            src_ref=leaving.at[pair], dst_ref=came.at[step + 1, pair], send_sem=block_sent.at[pair],
            recv_sem=block_came.at[step, pair], device_id=(row, partner(step)), device_id_type=MESH)

    def others(function):
        def one(shift, _):
            function((row + shift) % pairs)
            return 0

        lax.fori_loop(1, pairs, one, 0)

    def neighbours(function):
        def one(shift, _):
            function(plane + (row - plane + shift) % half)
            return 0

        lax.fori_loop(1, half, one, 0)

    def gram_full(pair):
        high, low = split_two(jnp.concatenate([kept[pair], came[0, pair]], 0))
        gram = lax.dot_general(
            jnp.concatenate([low, high, high], 1), jnp.concatenate([high, low, high], 1),
            (((1,), (1,)), ((), ())), preferred_element_type=F32)

        @pl.when(pair == own)
        def _():
            pack_gram(gram, gram_in.at[row])

        @pl.when(pair != own)
        def _():
            pack_gram(gram, gram_out.at[pair])
            gram_copy(pair).start()

    def gram_cross(step, pair):
        block_copy(step - 1, pair).wait_recv()
        high, low = split_two(kept[pair])
        came_high, came_low = split_two(came[step, pair])
        cross = lax.dot_general(
            jnp.concatenate([low, high, high], 1), jnp.concatenate([came_high, came_low, came_high], 1),
            (((1,), (1,)), ((), ())), preferred_element_type=F32)
        cross = jnp.concatenate([cross, jnp.zeros((BW, 128 - BW), F32)], 1)

        @pl.when(pair == own)
        def _():
            cross_in[step, row] = cross

        @pl.when(pair != own)
        def _():
            cross_out[pair] = cross
            cross_copy(step, pair).start()

    def gram_whole():
        others(lambda source: gram_arrival(source).wait_recv())
        total = gram_in[0]
        for source in range(1, pairs):
            total = total + gram_in[source]
        g_ref[:, :W] = unpack_gram(total)

    def gram_joined(step):
        others(lambda source: cross_arrival(step, source).wait_recv())
        diag_copy(step - 1).wait_recv()
        total = cross_in[step, 0]
        for source in range(1, pairs):
            total = total + cross_in[step, source]
        cross = total[:, :BW]
        g_ref[0:BW, :W] = jnp.concatenate([diag_kept[:, :BW], cross], 1)
        g_ref[BW:W, :W] = jnp.concatenate([jnp.transpose(cross), diag_in[step - 1][:, :BW]], 1)

    def own_rotation(step):
        came_first = (step > 0) & (slot_ref[jnp.maximum(step - 1, 0), own] == 0)
        gram = g_ref[:, :W]
        gram = jnp.where(came_first, swap_columns(swap_rows(gram)), gram)

        def ready(part):
            turned = e_ref[BW * part : BW * part + BW, :W]
            high, low = split_two(jnp.where(came_first, swap_columns(turned), turned))
            pack_half(high.astype(F32) + low.astype(F32), turn.at[step, own, part])
            turn_copy(step, part, own, across).start()
            neighbours(lambda target: turn_copy(step, part, own, target).start())

        rotate(gram, a_ref, e_ref, 32, ready)

    def turned_of(step, pair):
        halves = [unpack_half(turn[step, pair, part]) for part in range(2)]
        sent_first = slot_ref[step, pair] == 0
        return jnp.concatenate(
            [jnp.where(sent_first, halves[1], halves[0]), jnp.where(sent_first, halves[0], halves[1])], 0)

    def own_diagonals(step):
        turned = turned_of(step, own)
        exact = dict(precision=lax.Precision.HIGHEST, preferred_element_type=F32)
        product = lax.dot_general(turned, g_ref[:, :W], (((1,), (0,)), ((), ())), **exact)
        blank = jnp.zeros((BW, 128 - BW), F32)
        nt = (((1,), (1,)), ((), ()))
        stays = lax.dot_general(product[:BW], turned[:BW], nt, **exact)
        leaves = lax.dot_general(product[BW:], turned[BW:], nt, **exact)
        diag_kept[...] = jnp.concatenate([stays, blank], 1)
        diag_out[step] = jnp.concatenate([leaves, blank], 1)
        diag_copy(step).start()

    def update_one(step, pair):
        @pl.when((pair != own) & (pair != beyond))
        def _():
            turn_arrival(step, 0, pair).wait_recv()
            turn_arrival(step, 1, pair).wait_recv()

        @pl.when(pair != own)
        def _():
            @pl.when(step == 0)
            def _():
                gram_copy(pair).wait_send()

            @pl.when(step > 0)
            def _():
                cross_copy(step, pair).wait_send()

        @pl.when(step > 0)
        def _():
            block_copy(step - 1, pair).wait_send()

        turn_high, turn_low = split_two(turned_of(step, pair))
        high, low = split_two(jnp.concatenate([kept[pair], came[step, pair]], 0))
        dims = (((1,), (0,)), ((), ()))
        new = (
            lax.dot_general(turn_low, high, dims, preferred_element_type=F32)
            + lax.dot_general(turn_high, low, dims, preferred_element_type=F32)
            + lax.dot_general(turn_high, high, dims, preferred_element_type=F32))
        kept[pair] = new[0:BW]
        leaving[pair] = new[BW:]
        block_copy(step, pair).start()

    def phase(index, _):
        split = jnp.minimum(index // 2, 1)
        step = (1 - split) * index + split * (2 + (index - 2) // 2)
        start = split * half * (index % 2)
        count = pairs - split * half
        mine = (own >= start) & (own < start + count)

        def gram_one(i, _):
            pair = ordered(start, i)

            @pl.when(step == 0)
            def _():
                gram_full(pair)

            @pl.when(step > 0)
            def _():
                gram_cross(step, pair)

            return 0

        lax.fori_loop(0, count, gram_one, 0)

        @pl.when(mine)
        def _():
            @pl.when(step == 0)
            def _():
                gram_whole()

            @pl.when(step > 0)
            def _():
                gram_joined(step)

            own_rotation(step)

            def pass_on(part):
                turn_arrival(step, part, beyond).wait_recv()
                neighbours(lambda target: turn_copy(step, part, beyond, target).start())

            pass_on(0)

            @pl.when(step < STEPS - 1)
            def _():
                own_diagonals(step)

            pass_on(1)

        def update_next(i, _):
            update_one(step, ordered(start, i))
            return 0

        lax.fori_loop(0, count, update_next, 0)

        @pl.when(mine)
        def _():
            @pl.when(step < STEPS - 1)
            def _():
                diag_copy(step).wait_send()

            for part in range(2):
                turn_copy(step, part, own, across).wait_send()
                neighbours(lambda target: turn_copy(step, part, own, target).wait_send())
                neighbours(lambda target: turn_copy(step, part, beyond, target).wait_send())

        return 0

    lax.fori_loop(0, 6, phase, 0)

    def store(which, pair, index):
        source, target = ((kept.at[pair], kept_out), (came.at[STEPS, pair], came_out))[which]
        rows = pl.ds(pl.multiple_of(index * chunk, chunk), chunk)
        return pltpu.make_async_copy(source.at[:, rows], target.at[index, pair], local_sem.at[which, pair, index])

    def each(function):
        def one(i, _):
            function(i // chunks, i % chunks)
            return 0

        lax.fori_loop(0, pairs * chunks, one, 0)

    each(lambda pair, index: store(0, pair, index).start())

    def finish(i, _):
        pair = ordered(0, i)
        block_copy(STEPS - 1, pair).wait()
        for index in range(chunks):
            store(1, pair, index).start()
        return 0

    lax.fori_loop(0, pairs, finish, 0)
    for which in range(2):
        each(lambda pair, index: store(which, pair, index).wait())


def pair_steps(send_slot, block_order, hessian):
    rows, columns = hessian.shape
    pairs, width, chunk = columns // W, BW, 256
    block = jax.ShapeDtypeStruct((rows // chunk, pairs, width, chunk), F32)
    dma = pltpu.SemaphoreType.DMA
    return pl.pallas_call(
        functools.partial(pair_kernel, pairs),
        out_shape=[block, block],
        in_specs=[
            pl.BlockSpec(memory_space=pltpu.SMEM),
            pl.BlockSpec(memory_space=pltpu.SMEM),
            pl.BlockSpec(memory_space=pl.ANY),
        ],
        out_specs=[pl.BlockSpec(memory_space=pl.ANY)] * 2,
        scratch_shapes=[
            pltpu.VMEM((rows, columns), F32),
            pltpu.VMEM((2 * pairs, width, chunk), F32),
            pltpu.VMEM((pairs, width, rows), F32),
            pltpu.VMEM((STEPS + 1, pairs, width, rows), F32),
            pltpu.VMEM((pairs, width, rows), F32),
            pltpu.VMEM((pairs, 256, 128), F32),
            pltpu.VMEM((pairs, 256, 128), F32),
            pltpu.VMEM((pairs, width, 128), F32),
            pltpu.VMEM((STEPS, pairs, width, 128), F32),
            pltpu.VMEM((STEPS, width, 128), F32),
            pltpu.VMEM((STEPS, width, 128), F32),
            pltpu.VMEM((width, 128), F32),
            pltpu.VMEM((STEPS, pairs, 2, 144, 128), F32),
            pltpu.VMEM((W, 256), F32),
            pltpu.VMEM((W, 256), F32),
            pltpu.VMEM((W, 256), F32),
            dma((pairs,)),
            dma((pairs,)),
            dma((pairs,)),
            dma((STEPS, pairs)),
            dma((STEPS,)),
            dma((STEPS,)),
            dma((2, 2, pairs)),
            dma((STEPS, pairs, 2)),
            dma((pairs,)),
            dma((STEPS, pairs)),
            dma((rows // chunk,)),
            dma((2, pairs, rows // chunk)),
        ],
        compiler_params=pltpu.CompilerParams(
            collective_id=0, has_side_effects=True, vmem_limit_bytes=VMEM_LIMIT),
        name="pair_steps",
    )(send_slot, block_order, hessian)


def scatter_kernel(slot_ref, kept_ref, came_ref, out_ref):
    for pair in range(0, kept_ref.shape[1], 2):
        parts = []
        for each in (pair, pair + 1):
            came_first = slot_ref[STEPS - 1, each] == 0
            kept, came = kept_ref[0, each], came_ref[0, each]
            parts += [jnp.where(came_first, came, kept), jnp.where(came_first, kept, came)]
        out_ref[:, 192 * pair : 192 * pair + 384] = jnp.transpose(jnp.concatenate(parts, 0))


def scattered(send_slot, kept, came):
    chunks, pairs, width, chunk = kept.shape
    spec = pl.BlockSpec((1, pairs, width, chunk), lambda i: (i, 0, 0, 0))
    return pl.pallas_call(
        scatter_kernel,
        grid=(chunks,),
        out_shape=jax.ShapeDtypeStruct((chunks * chunk, pairs * 2 * width), F32),
        in_specs=[pl.BlockSpec(memory_space=pltpu.SMEM), spec, spec],
        out_specs=pl.BlockSpec((chunk, pairs * 2 * width), lambda i: (i, 0)),
        compiler_params=pltpu.CompilerParams(vmem_limit_bytes=VMEM_LIMIT),
        name="scattered",
    )(send_slot, kept, came)


def body(hessian, block_order, send_slot):
    kept, came = pair_steps(send_slot, block_order, hessian)
    return scattered(send_slot, kept, came)


def solution(mesh):
    in_specs = (P("row", "col"), P("col", None), P(None, "col"))
    out_specs = P("row", "col")
    return jax.shard_map(body, mesh=mesh, in_specs=in_specs, out_specs=out_specs, check_vma=False)
```

```python
import functools

import jax
import jax.numpy as jnp
from jax import lax
from jax.experimental import pallas as pl
from jax.experimental.pallas import tpu as pltpu
from jax.sharding import PartitionSpec as P

MESH = pl.DeviceIdType.MESH
F32=jnp.float32; BF=jnp.bfloat16
W=192;BW=96
def pieces(x):
    h=x.astype(BF); r=x-h.astype(F32); m=r.astype(BF); l=(r-m.astype(F32)).astype(BF)
    return h,m,l
def outer(left, right):
    a0,a1,a2=pieces(left); b0,b1,b2=pieces(right)
    a=jnp.concatenate([a2,a0,a1,a1,a0,a0],0)
    b=jnp.concatenate([b0,b2,b1,b0,b1,b0],0)
    return lax.dot_general(a,b,(((0,),(0,)),((),())),preferred_element_type=F32)
def rsqrt(d):
    r=lax.rsqrt(d)
    return r*(1.5-0.5*d*r*r)
def recip(d):
    return 1.0/d
def eliminate(rows, base, NB):
    diag=rows[0][:,base:base+NB]
    cols=[jnp.broadcast_to(diag[:,c:c+1],(NB,128)) for c in range(NB)]
    idx=lax.broadcasted_iota(jnp.int32,(NB,128),0)
    rows=[[r[:,i:i+128] for i in range(0,r.shape[1],128)] for r in rows]
    scale=jnp.zeros((NB,128),F32)
    for c in range(NB):
        col=cols[c]
        d=jnp.broadcast_to(col[c:c+1],(NB,128))
        m=jnp.where(idx>c,col*recip(d),0.0)
        scale=jnp.where(idx==c,d,scale)
        for q in range(c+1,NB):
            cols[q]=cols[q]-m*jnp.broadcast_to(col[q:q+1],(NB,128))
        for g in rows:
            for i in range(len(g)):
                g[i]=g[i]-m*jnp.broadcast_to(g[i][c:c+1],(NB,128))
    scale=rsqrt(scale)
    return [jnp.concatenate([x*scale for x in g],1) if len(g)>1 else g[0]*scale for g in rows]
def factor(a_ref, e_ref, NB, ready=None):
    for t in range(W//NB):
        j=t*NB
        lo=(j//128)*128
        panel=[a_ref[j:j+NB,lo:]]
        if e_ref is not None: panel.append(e_ref[j:j+NB,:])
        out=eliminate(panel,j-lo,NB)
        u=out[0]
        ri=lax.broadcasted_iota(jnp.int32,u.shape,0)+(j-lo)
        ci=lax.broadcasted_iota(jnp.int32,u.shape,1)
        u=jnp.where(ci>=ri,u,0.0)
        a_ref[j:j+NB,lo:]=u
        if lo: a_ref[j:j+NB,:lo]=jnp.zeros((NB,lo),F32)
        if e_ref is not None: e_ref[j:j+NB,:]=out[1]
        if ready is not None and (j+NB)%BW==0: ready((j+NB)//BW-1)
        rem=W-j-NB
        if rem==0: break
        left=u[:,j+NB-lo:W-lo]
        a_ref[j+NB:W,lo:]=a_ref[j+NB:W,lo:]-outer(left,u)
        if e_ref is not None:
            e_ref[j+NB:W,:]=e_ref[j+NB:W,:]-outer(left,out[1])
def rotate(g, a_ref, e_ref, NB, ready):
    s=jnp.sum(jnp.sum(g*g,axis=0,keepdims=True),axis=1,keepdims=True)
    y=g/jnp.sqrt(s)
    yy=y[:,:W]
    a_ref[:,:W]=lax.dot_general(yy,yy,(((0,),(0,)),((),())),precision=lax.Precision.HIGHEST,preferred_element_type=F32)
    a_ref[:,W:]=jnp.zeros((W,256-W),F32)
    factor(a_ref,None,NB)
    u=a_ref[...]
    e_ref[...]=u
    uu=u[:,:W]
    a_ref[:,:W]=lax.dot_general(uu,uu,(((1,),(1,)),((),())),precision=lax.Precision.HIGHEST,preferred_element_type=F32)
    a_ref[:,W:]=jnp.zeros((W,256-W),F32)
    factor(a_ref,e_ref,NB,ready)
STEPS = 4
ROWS_LOCAL = 1024
VMEM_LIMIT = 60 * 2**20


def split_two(x):
    high = x.astype(BF)
    return high, (x - high.astype(F32)).astype(BF)


def pack_gram(gram, ref):
    ref[0:W, :] = gram[:, 0:128]
    ref[W : W + 64, :] = jnp.concatenate([gram[128:W, 128:W], jnp.zeros((64, 64), F32)], 1)


def unpack_gram(packed):
    right = jnp.concatenate([jnp.transpose(packed[128:W, :]), packed[W : W + 64, 0:64]], 0)
    return jnp.concatenate([packed[0:W, :], right], 1)


def swap_rows(x):
    return jnp.concatenate([x[BW:], x[:BW]], 0)


def swap_columns(x):
    return jnp.concatenate([x[:, BW:], x[:, :BW]], 1)


def pack_half(half, ref):
    ref[0:BW, :] = half[:, 0:128]
    ref[BW:, :] = jnp.concatenate([half[0:48, 128:W], half[48:BW, 128:W]], 1)


def unpack_half(packed):
    tail = packed[BW:, :]
    right = jnp.concatenate([tail[:, 0:64], tail[:, 64:128]], 0)
    return jnp.concatenate([packed[0:BW, :], right], 1)


def pair_kernel(
    pairs, slot_ref, order_ref, hessian_ref, kept_out, came_out,
    slab, turned, kept, came, leaving, gram_out, gram_in, cross_out, cross_in, diag_out, diag_in, diag_kept, turn,
    g_ref, a_ref, e_ref,
    gram_sent, gram_came, cross_sent, cross_came, diag_sent, diag_came, turn_sent, turn_came,
    block_sent, block_came, load_sem, local_sem,
):
    row = lax.axis_index("row")
    col = lax.axis_index("col")
    half = pairs // 2
    across = (row + half) % pairs
    plane = row // half * half
    own = row // 2 + half * (row % 2)
    beyond = across // 2 + half * (across % 2)

    def owner(pair):
        return 2 * (pair % half) + pair // half

    def ordered(start, i):
        return start + half * (i // half) + (row // 2 + half - i % half) % half

    def partner(step):
        stride = (step * step * step + 5 * step + 6) // 6
        return col + stride * (1 - 2 * ((col // stride) % 2))

    chunk = turned.shape[2]
    chunks = slab.shape[0] // chunk

    def load(index):
        rows = pl.ds(pl.multiple_of(index * chunk, chunk), chunk)
        return pltpu.make_async_copy(hessian_ref.at[rows], slab.at[rows], load_sem.at[index])

    for index in range(chunks):
        load(index).start()

    barrier = pltpu.get_barrier_semaphore()
    for shift in range(1, pairs):
        pl.semaphore_signal(barrier, inc=1, device_id=((row + shift) % pairs, col), device_id_type=MESH)
    for step in range(STEPS):
        pl.semaphore_signal(barrier, inc=1, device_id=(row, partner(step)), device_id_type=MESH)

    def gather(index, _):
        load(index).wait()
        rows = pl.ds(pl.multiple_of(index * chunk, chunk), chunk)
        for part in range(slab.shape[1] // 384):
            turned[4 * part : 4 * part + 4] = jnp.transpose(
                slab[rows, 384 * part : 384 * part + 384]).reshape(4, BW, chunk)
        for pair in range(pairs):
            kept[pair, :, rows] = turned[order_ref[0, 2 * pair]]
            came[0, pair, :, rows] = turned[order_ref[0, 2 * pair + 1]]
        return 0

    lax.fori_loop(0, chunks, gather, 0)
    pl.semaphore_wait(barrier, pairs - 1 + STEPS)

    def gram_copy(pair):
        return pltpu.make_async_remote_copy(
            src_ref=gram_out.at[pair], dst_ref=gram_in.at[row], send_sem=gram_sent.at[pair],
            recv_sem=gram_came.at[row], device_id=(owner(pair), col), device_id_type=MESH)

    def gram_arrival(source):
        return pltpu.make_async_remote_copy(
            src_ref=gram_out.at[source], dst_ref=gram_in.at[source], send_sem=gram_sent.at[source],
            recv_sem=gram_came.at[source], device_id=(source, col), device_id_type=MESH)

    def cross_copy(step, pair):
        return pltpu.make_async_remote_copy(
            src_ref=cross_out.at[pair], dst_ref=cross_in.at[step, row], send_sem=cross_sent.at[pair],
            recv_sem=cross_came.at[step, row], device_id=(owner(pair), col), device_id_type=MESH)

    def cross_arrival(step, source):
        return pltpu.make_async_remote_copy(
            src_ref=cross_out.at[source], dst_ref=cross_in.at[step, source], send_sem=cross_sent.at[source],
            recv_sem=cross_came.at[step, source], device_id=(source, col), device_id_type=MESH)

    def diag_copy(step):
        return pltpu.make_async_remote_copy(
            src_ref=diag_out.at[step], dst_ref=diag_in.at[step], send_sem=diag_sent.at[step],
            recv_sem=diag_came.at[step], device_id=(row, partner(step)), device_id_type=MESH)

    def turn_copy(step, part, pair, target):
        return pltpu.make_async_remote_copy(
            src_ref=turn.at[step, pair, part], dst_ref=turn.at[step, pair, part],
            send_sem=turn_sent.at[part, pair // 2 % 2, target], recv_sem=turn_came.at[step, pair, part],
            device_id=(target, col), device_id_type=MESH)

    def turn_arrival(step, part, pair):
        return pltpu.make_async_remote_copy(
            src_ref=turn.at[step, pair, part], dst_ref=turn.at[step, pair, part],
            send_sem=turn_sent.at[part, 0, 0], recv_sem=turn_came.at[step, pair, part],
            device_id=(across, col), device_id_type=MESH)

    def block_copy(step, pair):
        return pltpu.make_async_remote_copy(
            src_ref=leaving.at[pair], dst_ref=came.at[step + 1, pair], send_sem=block_sent.at[pair],
            recv_sem=block_came.at[step, pair], device_id=(row, partner(step)), device_id_type=MESH)

    def others(function):
        def one(shift, _):
            function((row + shift) % pairs)
            return 0

        lax.fori_loop(1, pairs, one, 0)

    def neighbours(function):
        def one(shift, _):
            function(plane + (row - plane + shift) % half)
            return 0

        lax.fori_loop(1, half, one, 0)

    def gram_full(pair):
        high, low = split_two(jnp.concatenate([kept[pair], came[0, pair]], 0))
        gram = lax.dot_general(
            jnp.concatenate([low, high, high], 1), jnp.concatenate([high, low, high], 1),
            (((1,), (1,)), ((), ())), preferred_element_type=F32)

        @pl.when(pair == own)
        def _():
            pack_gram(gram, gram_in.at[row])

        @pl.when(pair != own)
        def _():
            pack_gram(gram, gram_out.at[pair])
            gram_copy(pair).start()

    def gram_cross(step, pair):
        block_copy(step - 1, pair).wait_recv()
        high, low = split_two(kept[pair])
        came_high, came_low = split_two(came[step, pair])
        cross = lax.dot_general(
            jnp.concatenate([low, high, high], 1), jnp.concatenate([came_high, came_low, came_high], 1),
            (((1,), (1,)), ((), ())), preferred_element_type=F32)
        cross = jnp.concatenate([cross, jnp.zeros((BW, 128 - BW), F32)], 1)

        @pl.when(pair == own)
        def _():
            cross_in[step, row] = cross

        @pl.when(pair != own)
        def _():
            cross_out[pair] = cross
            cross_copy(step, pair).start()

    def gram_whole():
        others(lambda source: gram_arrival(source).wait_recv())
        total = gram_in[0]
        for source in range(1, pairs):
            total = total + gram_in[source]
        g_ref[:, :W] = unpack_gram(total)

    def gram_joined(step):
        others(lambda source: cross_arrival(step, source).wait_recv())
        diag_copy(step - 1).wait_recv()
        total = cross_in[step, 0]
        for source in range(1, pairs):
            total = total + cross_in[step, source]
        cross = total[:, :BW]
        g_ref[0:BW, :W] = jnp.concatenate([diag_kept[:, :BW], cross], 1)
        g_ref[BW:W, :W] = jnp.concatenate([jnp.transpose(cross), diag_in[step - 1][:, :BW]], 1)

    def own_rotation(step):
        came_first = (step > 0) & (slot_ref[jnp.maximum(step - 1, 0), own] == 0)
        gram = g_ref[:, :W]
        gram = jnp.where(came_first, swap_columns(swap_rows(gram)), gram)

        def ready(part):
            turned = e_ref[BW * part : BW * part + BW, :W]
            high, low = split_two(jnp.where(came_first, swap_columns(turned), turned))
            pack_half(high.astype(F32) + low.astype(F32), turn.at[step, own, part])
            turn_copy(step, part, own, across).start()
            neighbours(lambda target: turn_copy(step, part, own, target).start())

        rotate(gram, a_ref, e_ref, 32, ready)

    def turned_of(step, pair):
        halves = [unpack_half(turn[step, pair, part]) for part in range(2)]
        sent_first = slot_ref[step, pair] == 0
        return jnp.concatenate(
            [jnp.where(sent_first, halves[1], halves[0]), jnp.where(sent_first, halves[0], halves[1])], 0)

    def own_diagonals(step):
        turned = turned_of(step, own)
        exact = dict(precision=lax.Precision.HIGHEST, preferred_element_type=F32)
        product = lax.dot_general(turned, g_ref[:, :W], (((1,), (0,)), ((), ())), **exact)
        blank = jnp.zeros((BW, 128 - BW), F32)
        nt = (((1,), (1,)), ((), ()))
        stays = lax.dot_general(product[:BW], turned[:BW], nt, **exact)
        leaves = lax.dot_general(product[BW:], turned[BW:], nt, **exact)
        diag_kept[...] = jnp.concatenate([stays, blank], 1)
        diag_out[step] = jnp.concatenate([leaves, blank], 1)
        diag_copy(step).start()

    def update_one(step, pair):
        @pl.when((pair != own) & (pair != beyond))
        def _():
            turn_arrival(step, 0, pair).wait_recv()
            turn_arrival(step, 1, pair).wait_recv()

        @pl.when(pair != own)
        def _():
            @pl.when(step == 0)
            def _():
                gram_copy(pair).wait_send()

            @pl.when(step > 0)
            def _():
                cross_copy(step, pair).wait_send()

        @pl.when(step > 0)
        def _():
            block_copy(step - 1, pair).wait_send()

        turn_high, turn_low = split_two(turned_of(step, pair))
        high, low = split_two(jnp.concatenate([kept[pair], came[step, pair]], 0))
        dims = (((1,), (0,)), ((), ()))
        new = (
            lax.dot_general(turn_low, high, dims, preferred_element_type=F32)
            + lax.dot_general(turn_high, low, dims, preferred_element_type=F32)
            + lax.dot_general(turn_high, high, dims, preferred_element_type=F32))
        kept[pair] = new[0:BW]
        leaving[pair] = new[BW:]

        @pl.when((step != 1) | (pair < half))
        def _():
            block_copy(step, pair).start()

    def phase(index, _):
        split = jnp.minimum(index // 2, 1)
        step = (1 - split) * index + split * (2 + (index - 2) // 2)
        start = split * half * (index % 2)
        count = pairs - split * half
        mine = (own >= start) & (own < start + count)

        def gram_one(i, _):
            pair = ordered(start, i)

            @pl.when(step == 0)
            def _():
                gram_full(pair)

            @pl.when(step > 0)
            def _():
                gram_cross(step, pair)

            return 0

        lax.fori_loop(0, count, gram_one, 0)

        @pl.when((step == 2) & (start == 0))
        def _():
            def held_back(i, _):
                block_copy(1, ordered(half, i)).start()
                return 0

            lax.fori_loop(0, half, held_back, 0)

        @pl.when(mine)
        def _():
            @pl.when(step == 0)
            def _():
                gram_whole()

            @pl.when(step > 0)
            def _():
                gram_joined(step)

            own_rotation(step)

            def pass_on(part):
                turn_arrival(step, part, beyond).wait_recv()
                neighbours(lambda target: turn_copy(step, part, beyond, target).start())

            pass_on(0)

            @pl.when(step < STEPS - 1)
            def _():
                own_diagonals(step)

            pass_on(1)

        def update_next(i, _):
            update_one(step, ordered(start, i))
            return 0

        lax.fori_loop(0, count, update_next, 0)

        @pl.when(mine)
        def _():
            @pl.when(step < STEPS - 1)
            def _():
                diag_copy(step).wait_send()

            for part in range(2):
                turn_copy(step, part, own, across).wait_send()
                neighbours(lambda target: turn_copy(step, part, own, target).wait_send())
                neighbours(lambda target: turn_copy(step, part, beyond, target).wait_send())

        return 0

    lax.fori_loop(0, 6, phase, 0)

    def store(which, pair, index):
        source, target = ((kept.at[pair], kept_out), (came.at[STEPS, pair], came_out))[which]
        rows = pl.ds(pl.multiple_of(index * chunk, chunk), chunk)
        return pltpu.make_async_copy(source.at[:, rows], target.at[index, pair], local_sem.at[which, pair, index])

    def each(function):
        def one(i, _):
            function(i // chunks, i % chunks)
            return 0

        lax.fori_loop(0, pairs * chunks, one, 0)

    each(lambda pair, index: store(0, pair, index).start())

    def finish(i, _):
        pair = ordered(0, i)
        block_copy(STEPS - 1, pair).wait()
        for index in range(chunks):
            store(1, pair, index).start()
        return 0

    lax.fori_loop(0, pairs, finish, 0)
    for which in range(2):
        each(lambda pair, index: store(which, pair, index).wait())


def pair_steps(send_slot, block_order, hessian):
    rows, columns = hessian.shape
    pairs, width, chunk = columns // W, BW, 256
    block = jax.ShapeDtypeStruct((rows // chunk, pairs, width, chunk), F32)
    dma = pltpu.SemaphoreType.DMA
    return pl.pallas_call(
        functools.partial(pair_kernel, pairs),
        out_shape=[block, block],
        in_specs=[
            pl.BlockSpec(memory_space=pltpu.SMEM),
            pl.BlockSpec(memory_space=pltpu.SMEM),
            pl.BlockSpec(memory_space=pl.ANY),
        ],
        out_specs=[pl.BlockSpec(memory_space=pl.ANY)] * 2,
        scratch_shapes=[
            pltpu.VMEM((rows, columns), F32),
            pltpu.VMEM((2 * pairs, width, chunk), F32),
            pltpu.VMEM((pairs, width, rows), F32),
            pltpu.VMEM((STEPS + 1, pairs, width, rows), F32),
            pltpu.VMEM((pairs, width, rows), F32),
            pltpu.VMEM((pairs, 256, 128), F32),
            pltpu.VMEM((pairs, 256, 128), F32),
            pltpu.VMEM((pairs, width, 128), F32),
            pltpu.VMEM((STEPS, pairs, width, 128), F32),
            pltpu.VMEM((STEPS, width, 128), F32),
            pltpu.VMEM((STEPS, width, 128), F32),
            pltpu.VMEM((width, 128), F32),
            pltpu.VMEM((STEPS, pairs, 2, 144, 128), F32),
            pltpu.VMEM((W, 256), F32),
            pltpu.VMEM((W, 256), F32),
            pltpu.VMEM((W, 256), F32),
            dma((pairs,)),
            dma((pairs,)),
            dma((pairs,)),
            dma((STEPS, pairs)),
            dma((STEPS,)),
            dma((STEPS,)),
            dma((2, 2, pairs)),
            dma((STEPS, pairs, 2)),
            dma((pairs,)),
            dma((STEPS, pairs)),
            dma((rows // chunk,)),
            dma((2, pairs, rows // chunk)),
        ],
        compiler_params=pltpu.CompilerParams(
            collective_id=0, has_side_effects=True, vmem_limit_bytes=VMEM_LIMIT),
        name="pair_steps",
    )(send_slot, block_order, hessian)


def scatter_kernel(slot_ref, kept_ref, came_ref, out_ref):
    for pair in range(0, kept_ref.shape[1], 2):
        parts = []
        for each in (pair, pair + 1):
            came_first = slot_ref[STEPS - 1, each] == 0
            kept, came = kept_ref[0, each], came_ref[0, each]
            parts += [jnp.where(came_first, came, kept), jnp.where(came_first, kept, came)]
        out_ref[:, 192 * pair : 192 * pair + 384] = jnp.transpose(jnp.concatenate(parts, 0))


def scattered(send_slot, kept, came):
    chunks, pairs, width, chunk = kept.shape
    spec = pl.BlockSpec((1, pairs, width, chunk), lambda i: (i, 0, 0, 0))
    return pl.pallas_call(
        scatter_kernel,
        grid=(chunks,),
        out_shape=jax.ShapeDtypeStruct((chunks * chunk, pairs * 2 * width), F32),
        in_specs=[pl.BlockSpec(memory_space=pltpu.SMEM), spec, spec],
        out_specs=pl.BlockSpec((chunk, pairs * 2 * width), lambda i: (i, 0)),
        compiler_params=pltpu.CompilerParams(vmem_limit_bytes=VMEM_LIMIT),
        name="scattered",
    )(send_slot, kept, came)


def body(hessian, block_order, send_slot):
    kept, came = pair_steps(send_slot, block_order, hessian)
    return scattered(send_slot, kept, came)


def solution(mesh):
    in_specs = (P("row", "col"), P("col", None), P(None, "col"))
    out_specs = P("row", "col")
    return jax.shard_map(body, mesh=mesh, in_specs=in_specs, out_specs=out_specs, check_vma=False)
```
